32 devices in a mesh: row: 4 (over z), col: 8 (over y, x, core).
Axes of the slice: x: 2, y: 2, z: 4, core: 2. Of those that a mesh axis runs over, the one named last changes fastest.
Arguments:
- lam_tiles: bfloat16 [32, 64, 16, 128], P(('row', 'col')), may hold values from -6 to 6
- lam_ids: int32 [32, 64], P(('row', 'col')), may hold values from 0 to 255, as said below
- integrals: bfloat16 [4096, 32768], P('row', 'col'), may hold values from -0.125 to 0.125
Outputs:
- ladder: float32 [512, 4096], P('col', 'row')
The draws below stay inside these ranges and needn't reach their ends.
Inputs may be any that keep to these rules, and one draw needn't show every extreme that they name: `lam_ids`: within a group the 64 ids are distinct; at most 16 of them lie in one block of 32 consecutive ids, and every group has exactly 16 in one block, the same block for all groups.
All inputs are finite; a program needn't handle non-finite values.
Results may differ from the reference program's by a relative error of at most 0.0003.
Values may be sent and summed in bfloat16 or wider, within the bound.
No kernel may reach another device: no remote copies, remote signals or barrier semaphores. Data moves between devices by JAX's collectives and lax.ppermute only.
A program may use at most 128 MiB of HBM per device.

```python
import jax
import jax.numpy as jnp
from jax import lax

TILE = 128
PG = 16
KT_DEV = 32
CAP = 16
G = 32
S = 64
KT = 256
NAB = 4096


def draw_lam_ids(key, part):
    blocks = KT // KT_DEV
    key_hot, key_bias, key_noise, key_perm = jax.random.split(key, 4)
    hot = jax.random.randint(key_hot, (), 0, blocks)
    bias = jax.random.randint(key_bias, (blocks,), 0, 65536)
    bias = jnp.where(jnp.arange(blocks) == hot, 4194304, bias)
    noise = jax.random.randint(key_noise, (G, blocks, CAP), 0, 65536)
    score = (bias[None, :, None] + noise).reshape(G, blocks * CAP)
    score = score * (blocks * CAP) + jnp.arange(blocks * CAP, dtype=jnp.int32)[None, :]
    chosen = lax.top_k(score, S)[1].astype(jnp.int32)
    block = chosen // CAP
    slot = chosen % CAP
    ranks = jax.random.randint(key_perm, (G, blocks, KT_DEV), 0, 1048576) * KT_DEV + jnp.arange(KT_DEV, dtype=jnp.int32)
    order = jnp.argsort(ranks, axis=-1).astype(jnp.int32).reshape(G, blocks * KT_DEV)
    within = jnp.take_along_axis(order, block * KT_DEV + slot, axis=1)
    return (block * KT_DEV + within).astype(jnp.int32)


def steps_of(rng, shape, pieces, least, largest):
    loudness = 1.0
    for axis_at, blocks in pieces:
        draws = jax.random.uniform(jax.random.fold_in(jax.random.fold_in(rng, 6), axis_at), (blocks,), jnp.float32, least / len(pieces), largest / len(pieces))
        loudness = loudness * jnp.repeat(jnp.exp(draws), shape[axis_at] // blocks).reshape((-1,) + (1,) * (len(shape) - 1 - axis_at))
    return loudness


def gaussian(key, dims, deviation, reach, shards=(), kind=jnp.bfloat16):
    loudness = steps_of(key, dims, shards, -0.22, 0.18) if shards else 1.0
    entries = jax.random.normal(key, dims, jnp.float32) * deviation * loudness
    return jnp.minimum(jnp.maximum(entries, -reach), reach).astype(kind)


def setup_inputs(seed: int = 0) -> dict:
    splits = jax.random.split(jax.random.key(seed), 4)
    lam_tiles = gaussian(splits[0], (G, S, PG, TILE), 1.0, 6.0, ((0, 32),))
    lam_ids = draw_lam_ids(jax.random.fold_in(splits[3], 71), 0)
    integrals = gaussian(splits[2], (NAB, KT * TILE), (S * TILE // 4) ** -0.5, 0.125, ((0, 4), (1, 8)))
    return {"lam_tiles": lam_tiles, "lam_ids": lam_ids, "integrals": integrals}


def reference(lam_tiles, lam_ids, integrals):
    columns = integrals.reshape(integrals.shape[0], KT, TILE)

    def one_group(group_args):
        tiles, ids = group_args
        picked = jnp.take(columns, ids.astype(jnp.int32), axis=1)
        flat_cols = picked.reshape(picked.shape[0], S * TILE)
        flat_tiles = jnp.transpose(tiles, (1, 0, 2)).reshape(PG, S * TILE)
        product = lax.dot_general(flat_tiles, flat_cols, (((1,), (1,)), ((), ())), preferred_element_type=jnp.float32)
        return 0.5 * product

    result = lax.map(one_group, (lam_tiles, lam_ids))
    return result.reshape(G * PG, NAB)
```

```python
import functools

import jax
import jax.numpy as jnp
from jax import lax
from jax.experimental import pallas as pl
from jax.experimental.pallas import tpu as pltpu
from jax.sharding import PartitionSpec as P

CAP = 16

VMEM = pl.BlockSpec(memory_space=pltpu.VMEM)
SMEM = pl.BlockSpec(memory_space=pltpu.SMEM)
ANY = pl.BlockSpec(memory_space=pl.ANY)


def shift_of(size):
    assert size & (size - 1) == 0
    return size.bit_length() - 1


class Plan:
    def __init__(self, lam_tiles, integrals):
        self.n_row = lax.axis_size("row")
        self.n_col = lax.axis_size("col")
        g_dev, self.slots, self.pairs, self.tile = lam_tiles.shape
        assert g_dev == 1 and self.pairs == 16 and self.slots <= self.tile
        self.ab, self.cd = integrals.shape
        self.kt = self.cd // self.tile
        self.n_pair = self.n_col // 2
        self.per_row = self.n_col // self.n_row
        assert self.per_row % 2 == 0
        self.owned = self.n_col * self.pairs // self.per_row
        self.bucket = (CAP + 1) * self.pairs
        self.head = -(-(self.n_col + 1) // 16) * 16
        self.packed = self.slots * self.pairs + self.head


def pack_kernel(plan, ids, me, tiles, packed, *rest):
    outs, (buf, head, count, sem) = rest[: plan.n_pair], rest[plan.n_pair :]
    rows = plan.pairs
    body = pltpu.make_async_copy(tiles, packed.at[pl.ds(0, plan.slots * rows)], sem.at[0])
    body.start()
    head[...] = jnp.full(head.shape, plan.kt, jnp.int32)
    for m in range(plan.n_col):
        count[m] = 0
    lane = lax.broadcasted_iota(jnp.int32, (1, plan.tile), 1)
    col = me[1]

    def step(s, slot_row):
        tile_id = ids[0, s]
        m = (tile_id >> shift_of(plan.kt)) ^ col
        place = count[m]
        count[m] = place + 1
        at = pl.multiple_of(m * plan.bucket + place * rows, rows)
        buf[pl.ds(at, rows), :] = tiles[pl.ds(pl.multiple_of(s * rows, rows), rows), :]
        line = head[pl.ds(m, 1), :]
        head[pl.ds(m, 1), :] = jnp.where(lane == place, tile_id & (plan.kt - 1), line)
        return jnp.where(lane == s, m * CAP + place, slot_row)

    slot_row = lax.fori_loop(0, plan.slots, step, jnp.zeros((1, plan.tile), jnp.int32), unroll=8)
    head[plan.n_col : plan.n_col + 1, :] = slot_row
    heads = head[...].astype(jnp.float32)
    spread_heads(plan, heads, buf)
    copies = [body]
    top = buf.at[pl.ds(plan.n_col * plan.bucket, plan.head)]
    top[...] = heads.astype(jnp.bfloat16)
    copies.append(pltpu.make_async_copy(top, packed.at[pl.ds(plan.slots * rows, plan.head)], sem.at[1]))
    copies[-1].start()
    for i, out in enumerate(outs):
        part = buf.at[pl.ds(i * 2 * plan.bucket, 2 * plan.bucket)]
        copies.append(pltpu.make_async_copy(part, out, sem.at[2 + i]))
        copies[-1].start()
    for copy in copies:
        copy.wait()


def spread_heads(plan, heads, buf):
    for m in range(plan.n_col):
        line = jnp.broadcast_to(heads[m : m + 1, :], (plan.pairs, plan.tile))
        at = m * plan.bucket + CAP * plan.pairs
        buf[at : at + plan.pairs, :] = line.astype(jnp.bfloat16)


def pack(plan, ids, me, tiles):
    bf16 = jnp.bfloat16
    return pl.pallas_call(
        functools.partial(pack_kernel, plan),
        out_shape=[jax.ShapeDtypeStruct((plan.packed, plan.tile), bf16)]
        + [jax.ShapeDtypeStruct((2 * plan.bucket, plan.tile), bf16)] * plan.n_pair,
        in_specs=[SMEM, SMEM, VMEM],
        out_specs=[ANY] * (1 + plan.n_pair),
        scratch_shapes=[
            pltpu.VMEM((plan.n_col * plan.bucket + plan.head, plan.tile), bf16),
            pltpu.VMEM((plan.head, plan.tile), jnp.int32),
            pltpu.SMEM((plan.n_col,), jnp.int32),
            pltpu.SemaphoreType.DMA((2 + plan.n_pair,)),
        ],
        name="pack_tiles",
    )(ids, me, tiles)


def bucket_kernel(plan, packed, *rest):
    outs, (buf, line, places, sem) = rest[: plan.n_pair], rest[plan.n_pair :]
    rows = plan.pairs
    heads = packed[plan.slots * rows :, :].astype(jnp.float32)
    line[...] = jnp.broadcast_to(heads[plan.n_col : plan.n_col + 1, :], line.shape).astype(jnp.int32)
    copy = pltpu.make_async_copy(line, places, sem.at[0])
    copy.start()
    spread_heads(plan, heads, buf)
    copy.wait()

    def step(s, _):
        place = places[0, s]
        at = pl.multiple_of((place + (place >> shift_of(CAP))) * rows, rows)
        buf[pl.ds(at, rows), :] = packed[pl.ds(pl.multiple_of(s * rows, rows), rows), :]
        return 0

    lax.fori_loop(0, plan.slots, step, 0, unroll=8)
    copies = []
    for i, out in enumerate(outs):
        part = buf.at[pl.ds(i * 2 * plan.bucket, 2 * plan.bucket)]
        copies.append(pltpu.make_async_copy(part, out, sem.at[1 + i]))
        copies[-1].start()
    for copy in copies:
        copy.wait()


def bucket(plan, packed):
    bf16 = jnp.bfloat16
    return pl.pallas_call(
        functools.partial(bucket_kernel, plan),
        out_shape=[jax.ShapeDtypeStruct((2 * plan.bucket, plan.tile), bf16)] * plan.n_pair,
        in_specs=[VMEM],
        out_specs=[ANY] * plan.n_pair,
        scratch_shapes=[
            pltpu.VMEM((plan.n_col * plan.bucket, plan.tile), bf16),
            pltpu.VMEM((8, plan.tile), jnp.int32),
            pltpu.SMEM((8, plan.tile), jnp.int32),
            pltpu.SemaphoreType.DMA((1 + plan.n_pair,)),
        ],
        name="bucket_tiles",
    )(packed)


def build_kernel(plan, me, *rest):
    near, far, out, line, places, sem = rest[: plan.n_pair], *rest[plan.n_pair :]
    rows = plan.pairs
    sources = [(ref, 0, 2 * i) for i, ref in enumerate(near)]
    sources += [(far, i * plan.bucket, 2 * i + 1) for i in range(plan.n_pair)]
    for i, (ref, base, _) in enumerate(sources):
        at = base + CAP * rows
        line[i : i + 1, :] = ref[at : at + rows, :].astype(jnp.float32)[0:1, :].astype(jnp.int32)
    copy = pltpu.make_async_copy(line, places, sem)
    copy.start()
    out[...] = jnp.zeros(out.shape, out.dtype)
    copy.wait()
    col = me[1]
    for i, (ref, base, m) in enumerate(sources):
        to = pl.multiple_of((col ^ m) * rows, rows)
        for s in range(CAP):
            at = pl.multiple_of(places[i, s] * plan.tile, plan.tile)
            tile = ref[base + s * rows : base + (s + 1) * rows, :]
            out[pl.ds(to, rows), pl.ds(at, plan.tile)] = tile


def build(plan, me, near, far):
    first = pl.BlockSpec((plan.bucket, plan.tile), lambda i: (0, 0))
    whole = pl.BlockSpec(far.shape, lambda i: (0, 0))
    shape = (plan.n_col * plan.pairs, plan.cd + plan.tile)
    return pl.pallas_call(
        functools.partial(build_kernel, plan),
        out_shape=jax.ShapeDtypeStruct(shape, jnp.bfloat16),
        grid=(1,),
        in_specs=[SMEM] + [first] * plan.n_pair + [whole],
        out_specs=pl.BlockSpec(shape, lambda i: (0, 0)),
        scratch_shapes=[
            pltpu.VMEM((plan.n_col, plan.tile), jnp.int32),
            pltpu.SMEM((plan.n_col, plan.tile), jnp.int32),
            pltpu.SemaphoreType.DMA,
        ],
        name="build_rows",
    )(me, *near, far)


def product_kernel(plan, me, *rest):
    planes, (cols, keep, send, lam, total) = rest[: plan.n_row], rest[plan.n_row :]
    height = plan.n_col * plan.pairs

    @pl.when(pl.program_id(0) == 0)
    def _():
        for d, plane in enumerate(planes):
            lam[d * height : (d + 1) * height, :] = plane[...]

    total[...] = lax.dot_general(
        lam[...], cols[...], (((1,), (1,)), ((), ())), preferred_element_type=jnp.float32
    )
    row, col = me[0], me[1]
    core = col & 1
    for d in range(plan.n_row):
        for h in range(0, plan.per_row, 2):
            to = ((((row ^ d) * plan.per_row + h) ^ col) >> 1) * plan.owned
            to = pl.multiple_of(to, plan.owned)
            for out, side in ((keep, core), (send, 1 - core)):
                at = pl.multiple_of(d * height + (h + side) * plan.owned, plan.owned)
                out[pl.ds(to, plan.owned), :] = total[pl.ds(at, plan.owned), :]


def product(plan, me, planes, integrals, block=256):
    height = plan.n_col * plan.pairs
    half = plan.n_pair * plan.owned
    return pl.pallas_call(
        functools.partial(product_kernel, plan),
        out_shape=[jax.ShapeDtypeStruct((half, plan.ab), jnp.float32)] * 2,
        grid=(plan.ab // block,),
        in_specs=[SMEM]
        + [pl.BlockSpec((height, plan.cd), lambda i: (0, 0))] * plan.n_row
        + [pl.BlockSpec((block, plan.cd), lambda i: (i, 0))],
        out_specs=[pl.BlockSpec((half, block), lambda i: (0, i))] * 2,
        scratch_shapes=[
            pltpu.VMEM((plan.n_row * height, plan.cd), jnp.bfloat16),
            pltpu.VMEM((plan.n_row * height, block), jnp.float32),
        ],
        compiler_params=pltpu.CompilerParams(vmem_limit_bytes=56 * 1024 * 1024),
        name="product",
    )(me, *planes, integrals)


def swap(x, axis, m):
    return lax.ppermute(x, axis, [(i, i ^ m) for i in range(lax.axis_size(axis))])


def shards(lam_tiles, lam_ids, integrals):
    plan = Plan(lam_tiles, integrals)
    me = jnp.stack([lax.axis_index("row"), lax.axis_index("col")]).astype(jnp.int32)
    tiles = lam_tiles.reshape(plan.slots * plan.pairs, plan.tile)
    packed, *own = pack(plan, lam_ids, me, tiles)
    arrived = [swap(packed, "row", d) for d in range(1, plan.n_row)]
    planes = []
    for d in range(plan.n_row):
        parts = own if d == 0 else bucket(plan, arrived[d - 1])
        near = [parts[0]] + [swap(parts[m], "col", 2 * m) for m in range(1, plan.n_pair)]
        far = jnp.concatenate([part[plan.bucket :] for part in near], axis=0)
        planes.append(build(plan, me, near, swap(far, "col", 1)))
    keep, send = product(plan, me, planes, integrals)
    got = swap(send, "col", 1)
    both = [
        keep[m * plan.owned : (m + 1) * plan.owned] + got[m * plan.owned : (m + 1) * plan.owned]
        for m in range(plan.n_pair)
    ]
    out = both[0]
    for m in range(1, plan.n_pair):
        out = out + swap(both[m], "col", 2 * m)
    return 0.5 * out


def solution(mesh):
    return jax.shard_map(
        shards,
        mesh=mesh,
        in_specs=(P(("row", "col"), None, None, None), P(("row", "col"), None), P("row", "col")),
        out_specs=P("col", "row"),
        check_vma=False,
    )
```

```python
import functools

import jax
import jax.numpy as jnp
from jax import lax
from jax.experimental import pallas as pl
from jax.experimental.pallas import tpu as pltpu
from jax.sharding import PartitionSpec as P

CAP = 16

VMEM = pl.BlockSpec(memory_space=pltpu.VMEM)
HBM = pl.BlockSpec(memory_space=pltpu.HBM)


def shift_of(size):
    assert size & (size - 1) == 0
    return size.bit_length() - 1


class Plan:
    def __init__(self, lam_tiles, integrals):
        self.n_row = lax.axis_size("row")
        self.n_col = lax.axis_size("col")
        g_dev, self.slots, self.pairs, self.tile = lam_tiles.shape
        assert g_dev == 1 and self.pairs == 16 and self.slots <= self.tile
        self.ab, self.cd = integrals.shape
        self.kt = self.cd // self.tile
        self.n_pair = self.n_col // 2
        self.per_row = self.n_col // self.n_row
        assert self.per_row % 2 == 0
        self.owned = self.n_col * self.pairs // self.per_row
        self.height = self.n_col * self.pairs
        self.bucket = (CAP + 1) * self.pairs
        self.head = -(-(self.n_col + 1) // 16) * 16
        self.body = self.slots * self.pairs
        self.packed = self.body + self.head


def pack_kernel(plan, ids, tiles, packed, ids_row, buf, sem):
    load = pltpu.make_async_copy(tiles, buf.at[pl.ds(0, plan.body)], sem.at[0])
    load_ids = pltpu.make_async_copy(ids, ids_row, sem.at[1])
    load_ids.start()
    load.start()
    load_ids.wait()
    n = plan.slots
    row = jnp.broadcast_to(ids_row[...], (n, n))
    col = row.astype(jnp.float32).T.astype(jnp.int32)
    here, there = (lax.broadcasted_iota(jnp.int32, (n, n), i) for i in range(2))
    same = (row >> shift_of(plan.kt)) == (col >> shift_of(plan.kt))
    place_row = jnp.sum(jnp.where(same & (here < there), 1, 0), axis=0, keepdims=True)
    place_col = jnp.sum(jnp.where(same & (there < here), 1, 0), axis=1, keepdims=True)
    line = lax.broadcasted_iota(jnp.int32, (plan.head, n), 0)
    ids_line = jnp.broadcast_to(ids_row[...], (plan.head, n))
    block = ids_line >> shift_of(plan.kt)
    lane = lax.broadcasted_iota(jnp.int32, (n, plan.tile), 1)
    tile_at = lax.broadcasted_iota(jnp.int32, (n, plan.tile), 0)

    def spread(values, where):
        return lax.dot_general(
            values.astype(jnp.float32).astype(jnp.bfloat16),
            jnp.where(where, 1.0, 0.0).astype(jnp.bfloat16),
            (((1,), (0,)), ((), ())),
            preferred_element_type=jnp.float32,
        )

    missing = jnp.where(block == line, (ids_line & (plan.kt - 1)) - plan.kt, 0)
    places = spread(missing, place_col == lane) + plan.kt
    slot = jnp.where(line == plan.n_col, block * CAP + place_row, 0)
    slots = spread(slot, tile_at == lane)
    top = lax.broadcasted_iota(jnp.int32, (plan.head, plan.tile), 0)
    head = jnp.where(top == plan.n_col, slots, places)
    buf[plan.body :, :] = head.astype(jnp.bfloat16)
    load.wait()
    store = pltpu.make_async_copy(buf, packed, sem.at[0])
    store.start()
    store.wait()


def pack(plan, ids, tiles):
    return pl.pallas_call(
        functools.partial(pack_kernel, plan),
        out_shape=jax.ShapeDtypeStruct((plan.packed, plan.tile), jnp.bfloat16),
        in_specs=[HBM, HBM],
        out_specs=HBM,
        scratch_shapes=[
            pltpu.VMEM(ids.shape, jnp.int32),
            pltpu.VMEM((plan.packed, plan.tile), jnp.bfloat16),
            pltpu.SemaphoreType.DMA((2,)),
        ],
        compiler_params=pltpu.CompilerParams(vmem_limit_bytes=8 * 1024 * 1024),
        cost_estimate=cost(plan, 2 * plan.packed * plan.tile * 2),
        name="pack_tiles",
    )(ids, tiles)


def cost(plan, moved, flops=0):
    return pl.CostEstimate(flops=flops, bytes_accessed=moved, transcendentals=0)


def bucket_kernel(plan, count, *rest):
    packed, outs = rest[:count], rest[count : count + plan.n_pair]
    bodies, tops, buf, heads, line, places, sem = rest[count + plan.n_pair :]
    rows, piece = plan.pairs, count * plan.bucket
    loads = []
    for i, ref in enumerate(packed):
        top = tops.at[pl.ds(i * plan.head, plan.head)]
        loads.append(pltpu.make_async_copy(ref.at[pl.ds(plan.body, plan.head)], top, sem.at[2 * i]))
        loads[-1].start()
    for i, ref in enumerate(packed):
        body = bodies.at[pl.ds(i * plan.body, plan.body)]
        loads.append(pltpu.make_async_copy(ref.at[pl.ds(0, plan.body)], body, sem.at[2 * i + 1]))
        loads[-1].start()
    col = lax.axis_index("col")
    for i in range(count):
        loads[i].wait()
        head = tops[i * plan.head : (i + 1) * plan.head, :].astype(jnp.float32)
        heads[i * plan.head : (i + 1) * plan.head, :] = head
        slot = head[plan.n_col : plan.n_col + 1, :].astype(jnp.int32)
        m = (slot >> shift_of(CAP)) ^ col
        at = (m >> 1) * piece + i * plan.bucket + (slot & (CAP - 1)) * rows
        line[i : i + 1, :] = jnp.where((m & 1) == 0, at, plan.n_pair * piece)
    copy = pltpu.make_async_copy(line, places, sem.at[2 * count])
    copy.start()
    for i in range(count):
        for chip in range(plan.n_pair):
            ids = heads[pl.ds(i * plan.head + (col ^ (2 * chip)), 1), :]
            at = chip * piece + i * plan.bucket + CAP * rows
            buf[at : at + rows, :] = jnp.broadcast_to(ids, (rows, plan.tile)).astype(jnp.bfloat16)
    copy.wait()
    for i in range(count):
        loads[count + i].wait()

        def step(s, _, i=i):
            at = pl.multiple_of(places[i, s], rows)
            tile = bodies[pl.ds(pl.multiple_of(i * plan.body + s * rows, rows), rows), :]
            buf[pl.ds(at, rows), :] = tile
            return 0

        lax.fori_loop(0, plan.slots, step, 0, unroll=16)
    copies = []
    for i, out in enumerate(outs):
        part = buf.at[pl.ds(i * piece, piece)]
        copies.append(pltpu.make_async_copy(part, out, sem.at[2 * count + 1 + i]))
        copies[-1].start()
    for copy in copies:
        copy.wait()


def bucket(plan, packed):
    count = len(packed)
    piece = count * plan.bucket
    lines = -(-count // 8) * 8
    bf16 = jnp.bfloat16
    return pl.pallas_call(
        functools.partial(bucket_kernel, plan, count),
        out_shape=[jax.ShapeDtypeStruct((piece, plan.tile), bf16)] * plan.n_pair,
        in_specs=[HBM] * count,
        out_specs=[HBM] * plan.n_pair,
        scratch_shapes=[
            pltpu.VMEM((count * plan.body, plan.tile), bf16),
            pltpu.VMEM((count * plan.head, plan.tile), bf16),
            pltpu.VMEM((plan.n_pair * piece + plan.pairs, plan.tile), bf16),
            pltpu.VMEM((count * plan.head, plan.tile), jnp.float32),
            pltpu.VMEM((lines, plan.tile), jnp.int32),
            pltpu.SMEM((lines, plan.tile), jnp.int32),
            pltpu.SemaphoreType.DMA((2 * count + 1 + plan.n_pair,)),
        ],
        compiler_params=pltpu.CompilerParams(vmem_limit_bytes=20 * 1024 * 1024),
        cost_estimate=cost(plan, 4 * plan.n_pair * piece * plan.tile * 2),
        name="bucket_tiles",
    )(*packed)


def stage_kernel(steps, block, source, out, sem):
    copies = []
    for i in range(steps):
        here = pl.ds(i * block, block)
        copies.append(pltpu.make_async_copy(source.at[here], out.at[here], sem.at[i]))
        copies[-1].start()
    for copy in copies:
        copy.wait()


def stage(plan, integrals, block=256):
    steps = plan.ab // block
    return pl.pallas_call(
        functools.partial(stage_kernel, steps, block),
        out_shape=pltpu.VMEM(integrals.shape, integrals.dtype),
        in_specs=[HBM],
        out_specs=VMEM,
        scratch_shapes=[pltpu.SemaphoreType.DMA((steps,))],
        compiler_params=pltpu.CompilerParams(vmem_limit_bytes=2 * 1024 * 1024),
        cost_estimate=cost(plan, 2 * plan.ab * plan.cd * 2),
        name="stage_integrals",
    )(integrals)


def send_kernel(plan, groups, block, *rest):
    n_in = len(groups) * plan.n_pair
    parts, rest = rest[:n_in], rest[n_in:]
    cols, lam, send, tiles, line, places, sem, part_sem = rest
    rows = plan.pairs
    half = plan.n_pair * plan.owned
    sources, loads, at = [], [], 0
    for g, planes in enumerate(groups):
        for chip in range(plan.n_pair):
            ref = parts[g * plan.n_pair + chip]
            to = tiles.at[pl.ds(at, ref.shape[0])]
            loads.append(pltpu.make_async_copy(ref, to, part_sem.at[len(loads)]))
            loads[-1].start()
            for d in planes:
                for side in range(2):
                    sources.append((at, d, 2 * chip + side))
                    at += plan.bucket
    lam[...] = jnp.zeros(lam.shape, lam.dtype)
    for load in loads:
        load.wait()
    for i, (base, _, _) in enumerate(sources):
        head = tiles[base + CAP * rows : base + plan.bucket, :].astype(jnp.float32)
        line[i : i + 1, :] = head[0:1, :].astype(jnp.int32)
    copy = pltpu.make_async_copy(line, places, sem)
    copy.start()
    copy.wait()
    row, col = lax.axis_index("row"), lax.axis_index("col")
    per_owner = plan.owned // rows
    for i, (base, d, m) in enumerate(sources):
        group = (row ^ d) * plan.n_col + (col ^ m)
        rel = (group >> shift_of(per_owner)) ^ col
        to = (rel & 1) * half + (rel >> 1) * plan.owned + (group & (per_owner - 1)) * rows
        for s in range(CAP):
            at = places[i, s]
            line_at = pl.multiple_of(jnp.where(at < plan.kt, to, 2 * half), rows)
            at = pl.multiple_of((at & (plan.kt - 1)) * plan.tile, plan.tile)
            tile = tiles[base + s * rows : base + (s + 1) * rows, :]
            lam[pl.ds(line_at, rows), pl.ds(at, plan.tile)] = tile
    multiply(plan, block, lam, half, cols, send)


def multiply(plan, block, lam, first, cols, out):
    for i in range(0, plan.ab, block):
        out[:, i : i + block] = lax.dot_general(
            lam[first : first + out.shape[0], :],
            cols[i : i + block, :],
            (((1,), (1,)), ((), ())),
            preferred_element_type=jnp.float32,
        )


def send_product(plan, groups, parts, integrals, block=256):
    half = plan.n_pair * plan.owned
    n_src = plan.n_row * plan.n_col
    flat = [part for group in parts for part in group]
    bf16 = jnp.bfloat16
    return pl.pallas_call(
        functools.partial(send_kernel, plan, groups, block),
        out_shape=[
            pltpu.VMEM((2 * half + plan.pairs, plan.cd), bf16),
            pltpu.VMEM((half, plan.ab), jnp.float32),
        ],
        in_specs=[HBM] * len(flat) + [VMEM],
        out_specs=[VMEM, VMEM],
        scratch_shapes=[
            pltpu.VMEM((n_src * plan.bucket, plan.tile), bf16),
            pltpu.VMEM((n_src, plan.tile), jnp.int32),
            pltpu.SMEM((n_src, plan.tile), jnp.int32),
            pltpu.SemaphoreType.DMA,
            pltpu.SemaphoreType.DMA((len(flat),)),
        ],
        compiler_params=pltpu.CompilerParams(vmem_limit_bytes=28 * 1024 * 1024),
        cost_estimate=cost(plan, plan.ab * plan.cd * 4, 4 * half * plan.ab * plan.cd),
        name="place_and_multiply",
    )(*flat, integrals)


def keep_kernel(plan, block, lam, cols, out):
    multiply(plan, block, lam, 0, cols, out)


def keep_product(plan, lam, integrals, block=256):
    half = plan.n_pair * plan.owned
    return pl.pallas_call(
        functools.partial(keep_kernel, plan, block),
        out_shape=pltpu.VMEM((half, plan.ab), jnp.float32),
        in_specs=[VMEM, VMEM],
        out_specs=VMEM,
        compiler_params=pltpu.CompilerParams(vmem_limit_bytes=20 * 1024 * 1024),
        cost_estimate=cost(plan, (plan.ab + half) * plan.cd * 2, 2 * half * plan.ab * plan.cd),
        name="multiply_kept",
    )(lam, integrals)


def swap(x, axis, m):
    return lax.ppermute(x, axis, [(i, i ^ m) for i in range(lax.axis_size(axis))])


def shards(lam_tiles, lam_ids, integrals):
    plan = Plan(lam_tiles, integrals)
    packed = pack(plan, lam_ids, lam_tiles.reshape(plan.body, plan.tile))
    groups = [[0], list(range(1, plan.n_row - 1)), [plan.n_row - 1]]
    parts = []

    def spread(planes):
        raws = [raw for d in planes for raw in (arrived[d], swap(arrived[d], "col", 1))]
        if len(parts) == 1:
            *raws, parts[0] = lax.optimization_barrier((*raws, parts[0]))
        elif parts:
            *raws, parts[-1][0] = lax.optimization_barrier((*raws, parts[-1][0]))
        out = bucket(plan, raws)
        parts.append([out[0]] + [swap(out[m], "col", 2 * m) for m in range(1, plan.n_pair)])

    arrived = {0: packed}
    bit = plan.n_row // 2
    arrived[bit] = swap(packed, "row", bit)
    spread(groups[0])
    staged = stage(plan, integrals)
    arrived[bit], parts[0][1], staged = lax.optimization_barrier((arrived[bit], parts[0][1], staged))
    while bit > 1:
        bit //= 2
        arrived.update({d | bit: swap(raw, "row", bit) for d, raw in arrived.items()})
    for group in groups[1:]:
        spread(group)
    lam, send = send_product(plan, groups, parts, staged)
    got = swap(send, "col", 1)
    keep = keep_product(plan, lam, staged)
    both = [
        keep[m * plan.owned : (m + 1) * plan.owned] + got[m * plan.owned : (m + 1) * plan.owned]
        for m in range(plan.n_pair)
    ]
    others = [swap(both[m], "col", 2 * m) for m in range(1, plan.n_pair)]
    return 0.5 * functools.reduce(jnp.add, others, both[0])


def solution(mesh):
    return jax.shard_map(
        shards,
        mesh=mesh,
        in_specs=(P(("row", "col"), None, None, None), P(("row", "col"), None), P("row", "col")),
        out_specs=P("col", "row"),
        check_vma=False,
    )
```

```python
import functools

import jax
import jax.numpy as jnp
from jax import lax
from jax.experimental import pallas as pl
from jax.experimental.pallas import tpu as pltpu
from jax.sharding import PartitionSpec as P

CAP = 16

VMEM = pl.BlockSpec(memory_space=pltpu.VMEM)
HBM = pl.BlockSpec(memory_space=pltpu.HBM)


def shift_of(size):
    assert size & (size - 1) == 0
    return size.bit_length() - 1


class Plan:
    def __init__(self, lam_tiles, integrals):
        self.n_row = lax.axis_size("row")
        self.n_col = lax.axis_size("col")
        g_dev, self.slots, self.pairs, self.tile = lam_tiles.shape
        assert g_dev == 1 and self.pairs == 16 and self.slots <= self.tile
        self.ab, self.cd = integrals.shape
        self.kt = self.cd // self.tile
        self.n_pair = self.n_col // 2
        self.per_row = self.n_col // self.n_row
        assert self.per_row % 2 == 0
        self.owned = self.n_col * self.pairs // self.per_row
        self.height = self.n_col * self.pairs
        self.bucket = (CAP + 1) * self.pairs
        self.head = -(-(self.n_col + 1) // 16) * 16
        self.body = self.slots * self.pairs
        self.packed = self.body + self.head


def pack_kernel(plan, ids, tiles, packed, ids_row, buf, sem):
    load = pltpu.make_async_copy(tiles, buf.at[pl.ds(0, plan.body)], sem.at[0])
    load_ids = pltpu.make_async_copy(ids, ids_row, sem.at[1])
    load_ids.start()
    load.start()
    load_ids.wait()
    n = plan.slots
    row = jnp.broadcast_to(ids_row[...], (n, n))
    col = row.astype(jnp.float32).T.astype(jnp.int32)
    here, there = (lax.broadcasted_iota(jnp.int32, (n, n), i) for i in range(2))
    same = (row >> shift_of(plan.kt)) == (col >> shift_of(plan.kt))
    place_row = jnp.sum(jnp.where(same & (here < there), 1, 0), axis=0, keepdims=True)
    place_col = jnp.sum(jnp.where(same & (there < here), 1, 0), axis=1, keepdims=True)
    line = lax.broadcasted_iota(jnp.int32, (plan.head, n), 0)
    ids_line = jnp.broadcast_to(ids_row[...], (plan.head, n))
    block = ids_line >> shift_of(plan.kt)
    lane = lax.broadcasted_iota(jnp.int32, (n, plan.tile), 1)
    tile_at = lax.broadcasted_iota(jnp.int32, (n, plan.tile), 0)

    def spread(values, where):
        return lax.dot_general(
            values.astype(jnp.float32).astype(jnp.bfloat16),
            jnp.where(where, 1.0, 0.0).astype(jnp.bfloat16),
            (((1,), (0,)), ((), ())),
            preferred_element_type=jnp.float32,
        )

    missing = jnp.where(block == line, (ids_line & (plan.kt - 1)) - plan.kt, 0)
    places = spread(missing, place_col == lane) + plan.kt
    slot = jnp.where(line == plan.n_col, block * CAP + place_row, 0)
    slots = spread(slot, tile_at == lane)
    top = lax.broadcasted_iota(jnp.int32, (plan.head, plan.tile), 0)
    head = jnp.where(top == plan.n_col, slots, places)
    buf[plan.body :, :] = head.astype(jnp.bfloat16)
    load.wait()
    store = pltpu.make_async_copy(buf, packed, sem.at[0])
    store.start()
    store.wait()


def pack(plan, ids, tiles):
    return pl.pallas_call(
        functools.partial(pack_kernel, plan),
        out_shape=jax.ShapeDtypeStruct((plan.packed, plan.tile), jnp.bfloat16),
        in_specs=[HBM, HBM],
        out_specs=HBM,
        scratch_shapes=[
            pltpu.VMEM(ids.shape, jnp.int32),
            pltpu.VMEM((plan.packed, plan.tile), jnp.bfloat16),
            pltpu.SemaphoreType.DMA((2,)),
        ],
        compiler_params=pltpu.CompilerParams(vmem_limit_bytes=8 * 1024 * 1024),
        cost_estimate=cost(plan, 2 * plan.packed * plan.tile * 2),
        name="pack_tiles",
    )(ids, tiles)


def cost(plan, moved, flops=0):
    return pl.CostEstimate(flops=flops, bytes_accessed=moved, transcendentals=0)


def bucket_kernel(plan, count, *rest):
    packed, (buf, bodies, tops, heads, line, places, sem) = rest[:count], rest[count:]
    rows, piece = plan.pairs, count * plan.bucket
    loads = []
    for i, ref in enumerate(packed):
        top = tops.at[pl.ds(i * plan.head, plan.head)]
        loads.append(pltpu.make_async_copy(ref.at[pl.ds(plan.body, plan.head)], top, sem.at[2 * i]))
        loads[-1].start()
    for i, ref in enumerate(packed):
        body = bodies.at[pl.ds(i * plan.body, plan.body)]
        loads.append(pltpu.make_async_copy(ref.at[pl.ds(0, plan.body)], body, sem.at[2 * i + 1]))
        loads[-1].start()
    col = lax.axis_index("col")
    for i in range(count):
        loads[i].wait()
        head = tops[i * plan.head : (i + 1) * plan.head, :].astype(jnp.float32)
        heads[i * plan.head : (i + 1) * plan.head, :] = head
        slot = head[plan.n_col : plan.n_col + 1, :].astype(jnp.int32)
        m = (slot >> shift_of(CAP)) ^ col
        at = (m >> 1) * piece + i * plan.bucket + (slot & (CAP - 1)) * rows
        line[i : i + 1, :] = jnp.where((m & 1) == 0, at, plan.n_pair * piece)
    copy = pltpu.make_async_copy(line, places, sem.at[2 * count])
    copy.start()
    for i in range(count):
        for chip in range(plan.n_pair):
            ids = heads[pl.ds(i * plan.head + (col ^ (2 * chip)), 1), :]
            at = chip * piece + i * plan.bucket + CAP * rows
            buf[at : at + rows, :] = jnp.broadcast_to(ids, (rows, plan.tile)).astype(jnp.bfloat16)
    copy.wait()
    for i in range(count):
        loads[count + i].wait()

        def step(s, _, i=i):
            at = pl.multiple_of(places[i, s], rows)
            tile = bodies[pl.ds(pl.multiple_of(i * plan.body + s * rows, rows), rows), :]
            buf[pl.ds(at, rows), :] = tile
            return 0

        lax.fori_loop(0, plan.slots, step, 0, unroll=16)


def bucket(plan, packed):
    count = len(packed)
    piece = count * plan.bucket
    lines = -(-count // 8) * 8
    bf16 = jnp.bfloat16
    out = pl.pallas_call(
        functools.partial(bucket_kernel, plan, count),
        out_shape=pltpu.VMEM((plan.n_pair * piece + plan.pairs, plan.tile), bf16),
        in_specs=[HBM] * count,
        out_specs=VMEM,
        scratch_shapes=[
            pltpu.VMEM((count * plan.body, plan.tile), bf16),
            pltpu.VMEM((count * plan.head, plan.tile), bf16),
            pltpu.VMEM((count * plan.head, plan.tile), jnp.float32),
            pltpu.VMEM((lines, plan.tile), jnp.int32),
            pltpu.SMEM((lines, plan.tile), jnp.int32),
            pltpu.SemaphoreType.DMA((2 * count + 1,)),
        ],
        compiler_params=pltpu.CompilerParams(vmem_limit_bytes=12 * 1024 * 1024),
        cost_estimate=cost(plan, 4 * plan.n_pair * piece * plan.tile * 2),
        name="bucket_tiles",
    )(*packed)
    return [out[i * piece : (i + 1) * piece] for i in range(plan.n_pair)]


def stage_kernel(steps, block, source, out, sem):
    copies = []
    for i in range(steps):
        here = pl.ds(i * block, block)
        copies.append(pltpu.make_async_copy(source.at[here], out.at[here], sem.at[i]))
        copies[-1].start()
    for copy in copies:
        copy.wait()


def stage(plan, integrals, block=256):
    steps = plan.ab // block
    return pl.pallas_call(
        functools.partial(stage_kernel, steps, block),
        out_shape=pltpu.VMEM(integrals.shape, integrals.dtype),
        in_specs=[HBM],
        out_specs=VMEM,
        scratch_shapes=[pltpu.SemaphoreType.DMA((steps,))],
        compiler_params=pltpu.CompilerParams(vmem_limit_bytes=2 * 1024 * 1024),
        cost_estimate=cost(plan, 2 * plan.ab * plan.cd * 2),
        name="stage_integrals",
    )(integrals)


def place(plan, planes, parts, lam, tiles, line, places, sem, part_sem):
    rows = plan.pairs
    half = plan.n_pair * plan.owned
    sources, loads, at = [], [], 0
    for ref, (chips, ds) in zip(parts, planes, strict=True):
        loads.append(pltpu.make_async_copy(ref, tiles.at[pl.ds(at, ref.shape[0])], part_sem.at[len(loads)]))
        loads[-1].start()
        for chip in chips:
            for d in ds:
                for side in range(2):
                    sources.append((at, d, 2 * chip + side))
                    at += plan.bucket
    yield
    for load in loads:
        load.wait()
    for i, (base, _, _) in enumerate(sources):
        head = tiles[base + CAP * rows : base + plan.bucket, :].astype(jnp.float32)
        line[i : i + 1, :] = head[0:1, :].astype(jnp.int32)
    copy = pltpu.make_async_copy(line, places, sem)
    copy.start()
    copy.wait()
    row, col = lax.axis_index("row"), lax.axis_index("col")
    per_owner = plan.owned // rows
    for i, (base, d, m) in enumerate(sources):
        group = (row ^ d) * plan.n_col + (col ^ m)
        rel = (group >> shift_of(per_owner)) ^ col
        to = (rel & 1) * half + (rel >> 1) * plan.owned + (group & (per_owner - 1)) * rows
        for s in range(CAP):
            at = places[i, s]
            line_at = pl.multiple_of(jnp.where(at < plan.kt, to, 2 * half), rows)
            at = pl.multiple_of((at & (plan.kt - 1)) * plan.tile, plan.tile)
            tile = tiles[base + s * rows : base + (s + 1) * rows, :]
            lam[pl.ds(line_at, rows), pl.ds(at, plan.tile)] = tile
    yield


def place_scratch(plan, planes):
    count = sum(2 * len(chips) * len(ds) for chips, ds in planes)
    lines = -(-count // 8) * 8
    return [
        pltpu.VMEM((count * plan.bucket, plan.tile), jnp.bfloat16),
        pltpu.VMEM((lines, plan.tile), jnp.int32),
        pltpu.SMEM((lines, plan.tile), jnp.int32),
        pltpu.SemaphoreType.DMA,
        pltpu.SemaphoreType.DMA((len(planes),)),
    ]


def lam_shape(plan):
    return pltpu.VMEM((2 * plan.n_pair * plan.owned + plan.pairs, plan.cd), jnp.bfloat16)


def early_kernel(plan, planes, *rest):
    parts, (lam, *scratch) = rest[: len(planes)], rest[len(planes) :]
    placing = place(plan, planes, parts, lam, *scratch)
    next(placing)
    lam[...] = jnp.zeros(lam.shape, lam.dtype)
    next(placing)


def place_early(plan, planes, parts):
    return pl.pallas_call(
        functools.partial(early_kernel, plan, planes),
        out_shape=lam_shape(plan),
        in_specs=[HBM] * len(parts),
        out_specs=VMEM,
        scratch_shapes=place_scratch(plan, planes),
        compiler_params=pltpu.CompilerParams(vmem_limit_bytes=12 * 1024 * 1024),
        cost_estimate=cost(plan, 8 * 1024 * 1024),
        name="place_early",
    )(*parts)


def send_kernel(plan, planes, block, _, cols, *rest):
    parts, (lam, send, *scratch) = rest[: len(planes)], rest[len(planes) :]
    placing = place(plan, planes, parts, lam, *scratch)
    next(placing)
    next(placing)
    multiply(plan, block, lam, plan.n_pair * plan.owned, cols, send)


def send_product(plan, lam, planes, parts, integrals, block=256):
    half = plan.n_pair * plan.owned
    return pl.pallas_call(
        functools.partial(send_kernel, plan, planes, block),
        out_shape=[lam_shape(plan), pltpu.VMEM((half, plan.ab), jnp.float32)],
        in_specs=[VMEM, VMEM] + [HBM] * len(parts),
        out_specs=[VMEM, VMEM],
        input_output_aliases={0: 0},
        scratch_shapes=place_scratch(plan, planes),
        compiler_params=pltpu.CompilerParams(vmem_limit_bytes=20 * 1024 * 1024),
        cost_estimate=cost(plan, plan.ab * plan.cd * 4, 4 * half * plan.ab * plan.cd),
        name="place_and_multiply",
    )(lam, integrals, *parts)


def multiply(plan, block, lam, first, cols, out):
    for i in range(0, plan.ab, block):
        out[:, i : i + block] = lax.dot_general(
            lam[first : first + out.shape[0], :],
            cols[i : i + block, :],
            (((1,), (1,)), ((), ())),
            preferred_element_type=jnp.float32,
        )


def keep_kernel(plan, block, lam, cols, out):
    multiply(plan, block, lam, 0, cols, out)


def keep_product(plan, lam, integrals, block=256):
    half = plan.n_pair * plan.owned
    return pl.pallas_call(
        functools.partial(keep_kernel, plan, block),
        out_shape=pltpu.VMEM((half, plan.ab), jnp.float32),
        in_specs=[VMEM, VMEM],
        out_specs=VMEM,
        compiler_params=pltpu.CompilerParams(vmem_limit_bytes=20 * 1024 * 1024),
        cost_estimate=cost(plan, (plan.ab + half) * plan.cd * 2, 2 * half * plan.ab * plan.cd),
        name="multiply_kept",
    )(lam, integrals)


def swap(x, axis, m):
    return lax.ppermute(x, axis, [(i, i ^ m) for i in range(lax.axis_size(axis))])


def shards(lam_tiles, lam_ids, integrals):
    plan = Plan(lam_tiles, integrals)
    packed = pack(plan, lam_ids, lam_tiles.reshape(plan.body, plan.tile))
    chips = range(plan.n_pair)

    def spread(ds):
        out = bucket(plan, [raw for d in ds for raw in (arrived[d], swap(arrived[d], "col", 1))])
        return [out[0]] + [swap(out[m], "col", 2 * m) for m in range(1, plan.n_pair)]

    bit = plan.n_row // 2
    arrived = {0: packed, bit: swap(packed, "row", bit)}
    own = spread([0])
    staged = stage(plan, integrals)
    arrived[bit], own, staged = lax.optimization_barrier((arrived[bit], own, staged))
    while bit > 1:
        bit //= 2
        arrived.update({d | bit: swap(raw, "row", bit) for d, raw in arrived.items() if d or bit > 1})
    *middle, last = sorted(arrived)[1:]
    early = spread(middle)
    arrived[last], early[0], own[0] = lax.optimization_barrier((arrived[last], early[0], own[0]))
    near = swap(jnp.concatenate(own, axis=0), "row", 1)
    late = spread([last])
    planes = [((chip,), (0,)) for chip in chips] + [((chip,), tuple(middle)) for chip in chips]
    lam = place_early(plan, planes, own + early)
    planes = [(chips, (1,))] + [((chip,), (last,)) for chip in chips]
    lam, send = send_product(plan, lam, planes, [near] + late, staged)
    got = swap(send, "col", 1)
    keep = keep_product(plan, lam, staged)
    both = [
        keep[m * plan.owned : (m + 1) * plan.owned] + got[m * plan.owned : (m + 1) * plan.owned]
        for m in range(plan.n_pair)
    ]
    others = [swap(both[m], "col", 2 * m) for m in range(1, plan.n_pair)]
    return 0.5 * functools.reduce(jnp.add, others, both[0])


def solution(mesh):
    return jax.shard_map(
        shards,
        mesh=mesh,
        in_specs=(P(("row", "col"), None, None, None), P(("row", "col"), None), P("row", "col")),
        out_specs=P("col", "row"),
        check_vma=False,
    )
```

```python
import functools

import jax
import jax.numpy as jnp
from jax import lax
from jax.experimental import pallas as pl
from jax.experimental.pallas import tpu as pltpu
from jax.sharding import PartitionSpec as P

CAP = 16

VMEM = pl.BlockSpec(memory_space=pltpu.VMEM)
HBM = pl.BlockSpec(memory_space=pltpu.HBM)


def shift_of(size):
    assert size & (size - 1) == 0
    return size.bit_length() - 1


class Plan:
    def __init__(self, lam_tiles, integrals):
        self.n_row = lax.axis_size("row")
        self.n_col = lax.axis_size("col")
        g_dev, self.slots, self.pairs, self.tile = lam_tiles.shape
        assert g_dev == 1 and self.pairs == 16 and self.slots <= self.tile
        self.ab, self.cd = integrals.shape
        self.kt = self.cd // self.tile
        self.n_pair = self.n_col // 2
        self.per_row = self.n_col // self.n_row
        assert self.per_row % 2 == 0
        self.owned = self.n_col * self.pairs // self.per_row
        self.height = self.n_col * self.pairs
        self.bucket = (CAP + 1) * self.pairs
        self.head = -(-(self.n_col + 1) // 16) * 16
        self.body = self.slots * self.pairs
        self.packed = self.body + self.head


def pack_kernel(plan, ids, tiles, packed, ids_row, buf, sem):
    load = pltpu.make_async_copy(tiles, buf.at[pl.ds(0, plan.body)], sem.at[0])
    load_ids = pltpu.make_async_copy(ids, ids_row, sem.at[1])
    load_ids.start()
    load.start()
    load_ids.wait()
    n = plan.slots
    row = jnp.broadcast_to(ids_row[...], (n, n))
    col = row.astype(jnp.float32).T.astype(jnp.int32)
    here, there = (lax.broadcasted_iota(jnp.int32, (n, n), i) for i in range(2))
    same = (row >> shift_of(plan.kt)) == (col >> shift_of(plan.kt))
    place_row = jnp.sum(jnp.where(same & (here < there), 1, 0), axis=0, keepdims=True)
    place_col = jnp.sum(jnp.where(same & (there < here), 1, 0), axis=1, keepdims=True)
    line = lax.broadcasted_iota(jnp.int32, (plan.head, n), 0)
    ids_line = jnp.broadcast_to(ids_row[...], (plan.head, n))
    block = ids_line >> shift_of(plan.kt)
    lane = lax.broadcasted_iota(jnp.int32, (n, plan.tile), 1)
    tile_at = lax.broadcasted_iota(jnp.int32, (n, plan.tile), 0)

    def spread(values, where):
        return lax.dot_general(
            values.astype(jnp.float32).astype(jnp.bfloat16),
            jnp.where(where, 1.0, 0.0).astype(jnp.bfloat16),
            (((1,), (0,)), ((), ())),
            preferred_element_type=jnp.float32,
        )

    missing = jnp.where(block == line, (ids_line & (plan.kt - 1)) - plan.kt, 0)
    places = spread(missing, place_col == lane) + plan.kt
    slot = jnp.where(line == plan.n_col, block * CAP + place_row, 0)
    slots = spread(slot, tile_at == lane)
    top = lax.broadcasted_iota(jnp.int32, (plan.head, plan.tile), 0)
    head = jnp.where(top == plan.n_col, slots, places)
    buf[plan.body :, :] = head.astype(jnp.bfloat16)
    load.wait()
    store = pltpu.make_async_copy(buf, packed, sem.at[0])
    store.start()
    store.wait()


def pack(plan, ids, tiles):
    return pl.pallas_call(
        functools.partial(pack_kernel, plan),
        out_shape=jax.ShapeDtypeStruct((plan.packed, plan.tile), jnp.bfloat16),
        in_specs=[HBM, HBM],
        out_specs=HBM,
        scratch_shapes=[
            pltpu.VMEM(ids.shape, jnp.int32),
            pltpu.VMEM((plan.packed, plan.tile), jnp.bfloat16),
            pltpu.SemaphoreType.DMA((2,)),
        ],
        compiler_params=pltpu.CompilerParams(vmem_limit_bytes=8 * 1024 * 1024),
        cost_estimate=cost(plan, 2 * plan.packed * plan.tile * 2),
        name="pack_tiles",
    )(ids, tiles)


def cost(plan, moved, flops=0):
    return pl.CostEstimate(flops=flops, bytes_accessed=moved, transcendentals=0)


def bucket_kernel(plan, count, *rest):
    packed, (buf, bodies, tops, heads, line, places, sem) = rest[:count], rest[count:]
    rows, piece = plan.pairs, count * plan.bucket
    loads = []
    for i, ref in enumerate(packed):
        top = tops.at[pl.ds(i * plan.head, plan.head)]
        loads.append(pltpu.make_async_copy(ref.at[pl.ds(plan.body, plan.head)], top, sem.at[2 * i]))
        loads[-1].start()
    for i, ref in enumerate(packed):
        body = bodies.at[pl.ds(i * plan.body, plan.body)]
        loads.append(pltpu.make_async_copy(ref.at[pl.ds(0, plan.body)], body, sem.at[2 * i + 1]))
        loads[-1].start()
    col = lax.axis_index("col")
    for i in range(count):
        loads[i].wait()
        head = tops[i * plan.head : (i + 1) * plan.head, :].astype(jnp.float32)
        heads[i * plan.head : (i + 1) * plan.head, :] = head
        slot = head[plan.n_col : plan.n_col + 1, :].astype(jnp.int32)
        m = (slot >> shift_of(CAP)) ^ col
        at = (m >> 1) * piece + i * plan.bucket + (slot & (CAP - 1)) * rows
        line[i : i + 1, :] = jnp.where((m & 1) == 0, at, plan.n_pair * piece)
    copy = pltpu.make_async_copy(line, places, sem.at[2 * count])
    copy.start()
    for i in range(count):
        for chip in range(plan.n_pair):
            ids = heads[pl.ds(i * plan.head + (col ^ (2 * chip)), 1), :]
            at = chip * piece + i * plan.bucket + CAP * rows
            buf[at : at + rows, :] = jnp.broadcast_to(ids, (rows, plan.tile)).astype(jnp.bfloat16)
    copy.wait()
    for i in range(count):
        loads[count + i].wait()

        def step(s, _, i=i):
            at = pl.multiple_of(places[i, s], rows)
            tile = bodies[pl.ds(pl.multiple_of(i * plan.body + s * rows, rows), rows), :]
            buf[pl.ds(at, rows), :] = tile
            return 0

        lax.fori_loop(0, plan.slots, step, 0, unroll=16)


def bucket(plan, packed):
    count = len(packed)
    piece = count * plan.bucket
    lines = -(-count // 8) * 8
    bf16 = jnp.bfloat16
    out = pl.pallas_call(
        functools.partial(bucket_kernel, plan, count),
        out_shape=pltpu.VMEM((plan.n_pair * piece + plan.pairs, plan.tile), bf16),
        in_specs=[HBM] * count,
        out_specs=VMEM,
        scratch_shapes=[
            pltpu.VMEM((count * plan.body, plan.tile), bf16),
            pltpu.VMEM((count * plan.head, plan.tile), bf16),
            pltpu.VMEM((count * plan.head, plan.tile), jnp.float32),
            pltpu.VMEM((lines, plan.tile), jnp.int32),
            pltpu.SMEM((lines, plan.tile), jnp.int32),
            pltpu.SemaphoreType.DMA((2 * count + 1,)),
        ],
        compiler_params=pltpu.CompilerParams(vmem_limit_bytes=12 * 1024 * 1024),
        cost_estimate=cost(plan, 4 * plan.n_pair * piece * plan.tile * 2),
        name="bucket_tiles",
    )(*packed)
    return [out[i * piece : (i + 1) * piece] for i in range(plan.n_pair)]


def stage_kernel(steps, block, source, out, sem):
    copies = []
    for i in range(steps):
        here = pl.ds(i * block, block)
        copies.append(pltpu.make_async_copy(source.at[here], out.at[here], sem.at[i]))
        copies[-1].start()
    for copy in copies:
        copy.wait()


def stage(plan, integrals, block=256):
    steps = plan.ab // block
    return pl.pallas_call(
        functools.partial(stage_kernel, steps, block),
        out_shape=pltpu.VMEM(integrals.shape, integrals.dtype),
        in_specs=[HBM],
        out_specs=VMEM,
        scratch_shapes=[pltpu.SemaphoreType.DMA((steps,))],
        compiler_params=pltpu.CompilerParams(vmem_limit_bytes=2 * 1024 * 1024),
        cost_estimate=cost(plan, 2 * plan.ab * plan.cd * 2),
        name="stage_integrals",
    )(integrals)


def place(plan, planes, parts, lam, tiles, line, places, sem, part_sem):
    rows = plan.pairs
    half = plan.n_pair * plan.owned
    sources, loads, at = [], [], 0
    for ref, (chips, ds) in zip(parts, planes, strict=True):
        loads.append(pltpu.make_async_copy(ref, tiles.at[pl.ds(at, ref.shape[0])], part_sem.at[len(loads)]))
        loads[-1].start()
        for chip in chips:
            for d in ds:
                for side in range(2):
                    sources.append((at, d, 2 * chip + side))
                    at += plan.bucket
    yield
    for load in loads:
        load.wait()
    for i, (base, _, _) in enumerate(sources):
        head = tiles[base + CAP * rows : base + plan.bucket, :].astype(jnp.float32)
        line[i : i + 1, :] = head[0:1, :].astype(jnp.int32)
    copy = pltpu.make_async_copy(line, places, sem)
    copy.start()
    copy.wait()
    row, col = lax.axis_index("row"), lax.axis_index("col")
    per_owner = plan.owned // rows
    for i, (base, d, m) in enumerate(sources):
        group = (row ^ d) * plan.n_col + (col ^ m)
        rel = (group >> shift_of(per_owner)) ^ col
        to = (rel & 1) * half + (rel >> 1) * plan.owned + (group & (per_owner - 1)) * rows
        for s in range(CAP):
            at = places[i, s]
            line_at = pl.multiple_of(jnp.where(at < plan.kt, to, 2 * half), rows)
            at = pl.multiple_of((at & (plan.kt - 1)) * plan.tile, plan.tile)
            tile = tiles[base + s * rows : base + (s + 1) * rows, :]
            lam[pl.ds(line_at, rows), pl.ds(at, plan.tile)] = tile
    yield


def place_scratch(plan, planes):
    count = sum(2 * len(chips) * len(ds) for chips, ds in planes)
    lines = -(-count // 8) * 8
    return [
        pltpu.VMEM((count * plan.bucket, plan.tile), jnp.bfloat16),
        pltpu.VMEM((lines, plan.tile), jnp.int32),
        pltpu.SMEM((lines, plan.tile), jnp.int32),
        pltpu.SemaphoreType.DMA,
        pltpu.SemaphoreType.DMA((len(planes),)),
    ]


def lam_shape(plan):
    return pltpu.VMEM((2 * plan.n_pair * plan.owned + plan.pairs, plan.cd), jnp.bfloat16)


def early_kernel(plan, planes, *rest):
    parts, (lam, *scratch) = rest[: len(planes)], rest[len(planes) :]
    placing = place(plan, planes, parts, lam, *scratch)
    next(placing)
    lam[...] = jnp.zeros(lam.shape, lam.dtype)
    next(placing)


def place_early(plan, planes, parts):
    return pl.pallas_call(
        functools.partial(early_kernel, plan, planes),
        out_shape=lam_shape(plan),
        in_specs=[HBM] * len(parts),
        out_specs=VMEM,
        scratch_shapes=place_scratch(plan, planes),
        compiler_params=pltpu.CompilerParams(vmem_limit_bytes=12 * 1024 * 1024),
        cost_estimate=cost(plan, 8 * 1024 * 1024),
        name="place_early",
    )(*parts)


def send_kernel(plan, planes, block, _, cols, *rest):
    parts, (lam, send, *scratch) = rest[: len(planes)], rest[len(planes) :]
    placing = place(plan, planes, parts, lam, *scratch)
    next(placing)
    next(placing)
    multiply(plan, block, lam, plan.n_pair * plan.owned, cols, send)


def send_product(plan, lam, planes, parts, integrals, block=256):
    half = plan.n_pair * plan.owned
    return pl.pallas_call(
        functools.partial(send_kernel, plan, planes, block),
        out_shape=[lam_shape(plan), pltpu.VMEM((half, plan.ab), jnp.float32)],
        in_specs=[VMEM, VMEM] + [HBM] * len(parts),
        out_specs=[VMEM, VMEM],
        input_output_aliases={0: 0},
        scratch_shapes=place_scratch(plan, planes),
        compiler_params=pltpu.CompilerParams(vmem_limit_bytes=20 * 1024 * 1024),
        cost_estimate=cost(plan, plan.ab * plan.cd * 4, 4 * half * plan.ab * plan.cd),
        name="place_and_multiply",
    )(lam, integrals, *parts)


def multiply(plan, block, lam, first, cols, out):
    for i in range(0, plan.ab, block):
        out[:, i : i + block] = lax.dot_general(
            lam[first : first + out.shape[0], :],
            cols[i : i + block, :],
            (((1,), (1,)), ((), ())),
            preferred_element_type=jnp.float32,
        )


def keep_kernel(plan, block, lam, cols, out):
    multiply(plan, block, lam, 0, cols, out)


def keep_product(plan, lam, integrals, block=256):
    half = plan.n_pair * plan.owned
    return pl.pallas_call(
        functools.partial(keep_kernel, plan, block),
        out_shape=pltpu.VMEM((half, plan.ab), jnp.float32),
        in_specs=[VMEM, VMEM],
        out_specs=VMEM,
        compiler_params=pltpu.CompilerParams(vmem_limit_bytes=20 * 1024 * 1024),
        cost_estimate=cost(plan, (plan.ab + half) * plan.cd * 2, 2 * half * plan.ab * plan.cd),
        name="multiply_kept",
    )(lam, integrals)


def chunks_of(plan):
    return plan.ab // plan.tile


def words_shape(plan):
    return (chunks_of(plan) // 2 * plan.owned + chunks_of(plan), plan.tile)


def raised(x, power):
    half = jnp.floor(power * 0.5)
    return x * jnp.exp2(half) * jnp.exp2(power - half)


def code_kernel(plan, keep, got, mine, *rest):
    words, square = rest[:-1], rest[-1]
    rows, tile, chunks = plan.owned, plan.tile, chunks_of(plan)
    lane = lax.broadcasted_iota(jnp.int32, (rows, tile), 1)
    mine[...] = keep[:rows, :] + got[:rows, :]
    square[...] = jnp.zeros(square.shape, jnp.float32)
    for m, out in enumerate(words, 1):
        here = slice(m * rows, (m + 1) * rows)
        cells = [slice(j * tile, (j + 1) * tile) for j in range(chunks)]
        sums = [keep[here, cell] + got[here, cell] for cell in cells]
        most = jnp.zeros((rows, tile), jnp.float32)
        for j, part in enumerate(sums):
            most = jnp.where(lane == j, jnp.max(jnp.abs(part), axis=1, keepdims=True), most)
        power = jnp.floor(jnp.log2(jnp.maximum(most, 2.0**-120)) + 1.001)
        square[:rows, :] = power
        counts = []
        for j, part in enumerate(sums):
            count = jnp.floor(raised(part, 15.0 - power[:, j : j + 1]) + 0.5)
            counts.append(jnp.clip(count, -32767.0, 32767.0).astype(jnp.int32))
        for j in range(chunks // 2):
            word = (counts[j] << 16) | (counts[j + chunks // 2] & 65535)
            out[j * rows : (j + 1) * rows, :] = word
        out[chunks // 2 * rows :, :] = square[...].T[:chunks, :].astype(jnp.int32)


def code_sums(plan, keep, got):
    block = pltpu.VMEM((plan.owned, plan.ab), jnp.float32)
    return pl.pallas_call(
        functools.partial(code_kernel, plan),
        out_shape=[block] + [pltpu.VMEM(words_shape(plan), jnp.int32)] * (plan.n_pair - 1),
        in_specs=[VMEM] * 2,
        out_specs=[VMEM] * plan.n_pair,
        scratch_shapes=[pltpu.VMEM((plan.tile, plan.tile), jnp.float32)],
        compiler_params=pltpu.CompilerParams(vmem_limit_bytes=20 * 1024 * 1024),
        cost_estimate=cost(plan, 4 * plan.n_pair * plan.owned * plan.ab * 4),
        name="code_sums",
    )(keep, got)


def total_kernel(plan, mine, *rest):
    words, (out, square) = rest[:-2], rest[-2:]
    rows, tile, chunks = plan.owned, plan.tile, chunks_of(plan)
    out[...] = mine[...]
    square[...] = jnp.zeros(square.shape, jnp.float32)
    for ref in words:
        square[:chunks, :] = ref[chunks // 2 * rows :, :].astype(jnp.float32)
        power = square[...].T[:rows, :] - 15.0
        for j in range(chunks):
            at = j % (chunks // 2) * rows
            word = ref[at : at + rows, :]
            count = (word if j < chunks // 2 else word << 16) >> 16
            cell = slice(j * tile, (j + 1) * tile)
            out[:, cell] += raised(count.astype(jnp.float32), power[:, j : j + 1])
    out[...] = 0.5 * out[...]


def total_sums(plan, mine, words):
    return pl.pallas_call(
        functools.partial(total_kernel, plan),
        out_shape=jax.ShapeDtypeStruct((plan.owned, plan.ab), jnp.float32),
        in_specs=[VMEM] * (1 + len(words)),
        out_specs=VMEM,
        scratch_shapes=[pltpu.VMEM((plan.tile, plan.tile), jnp.float32)],
        compiler_params=pltpu.CompilerParams(vmem_limit_bytes=20 * 1024 * 1024),
        cost_estimate=cost(plan, 4 * plan.n_pair * plan.owned * plan.ab * 4),
        name="total_sums",
    )(mine, *words)


def swap(x, axis, m):
    return lax.ppermute(x, axis, [(i, i ^ m) for i in range(lax.axis_size(axis))])


def shards(lam_tiles, lam_ids, integrals):
    plan = Plan(lam_tiles, integrals)
    packed = pack(plan, lam_ids, lam_tiles.reshape(plan.body, plan.tile))
    chips = range(plan.n_pair)

    def spread(ds):
        out = bucket(plan, [raw for d in ds for raw in (arrived[d], swap(arrived[d], "col", 1))])
        return [out[0]] + [swap(out[m], "col", 2 * m) for m in range(1, plan.n_pair)]

    bit = plan.n_row // 2
    arrived = {0: packed, bit: swap(packed, "row", bit)}
    own = spread([0])
    staged = stage(plan, integrals)
    arrived[bit], own, staged = lax.optimization_barrier((arrived[bit], own, staged))
    while bit > 1:
        bit //= 2
        arrived.update({d | bit: swap(raw, "row", bit) for d, raw in arrived.items() if d or bit > 1})
    *middle, last = sorted(arrived)[1:]
    early = spread(middle)
    arrived[last], early[1], own[0] = lax.optimization_barrier((arrived[last], early[1], own[0]))
    near = swap(jnp.concatenate(own, axis=0), "row", 1)
    late = spread([last])
    planes = [((chip,), (0,)) for chip in chips] + [((chip,), tuple(middle)) for chip in chips]
    lam = place_early(plan, planes, own + early)
    planes = [(chips, (1,))] + [((chip,), (last,)) for chip in chips]
    lam, send = send_product(plan, lam, planes, [near] + late, staged)
    got = swap(send, "col", 1)
    keep = keep_product(plan, lam, staged)
    mine, *words = code_sums(plan, keep, got)
    return total_sums(plan, mine, [swap(word, "col", 2 * m) for m, word in enumerate(words, 1)])


def solution(mesh):
    return jax.shard_map(
        shards,
        mesh=mesh,
        in_specs=(P(("row", "col"), None, None, None), P(("row", "col"), None), P("row", "col")),
        out_specs=P("col", "row"),
        check_vma=False,
    )
```

```python
import functools

import jax
import jax.numpy as jnp
from jax import lax
from jax.experimental import pallas as pl
from jax.experimental.pallas import tpu as pltpu
from jax.sharding import PartitionSpec as P

CAP = 16

VMEM = pl.BlockSpec(memory_space=pltpu.VMEM)
HBM = pl.BlockSpec(memory_space=pltpu.HBM)


def shift_of(size):
    assert size & (size - 1) == 0
    return size.bit_length() - 1


class Plan:
    def __init__(self, lam_tiles, integrals):
        self.n_row = lax.axis_size("row")
        self.n_col = lax.axis_size("col")
        g_dev, self.slots, self.pairs, self.tile = lam_tiles.shape
        assert g_dev == 1 and self.pairs == 16 and self.slots <= self.tile
        self.ab, self.cd = integrals.shape
        self.kt = self.cd // self.tile
        self.n_pair = self.n_col // 2
        self.per_row = self.n_col // self.n_row
        assert self.per_row % 2 == 0
        self.owned = self.n_col * self.pairs // self.per_row
        self.height = self.n_col * self.pairs
        self.bucket = (CAP + 1) * self.pairs
        self.head = -(-(self.n_col + 1) // 16) * 16
        self.body = self.slots * self.pairs
        self.packed = self.body + self.head


def pack_kernel(plan, ids, tiles, packed, ids_row, buf, sem):
    load = pltpu.make_async_copy(tiles, buf.at[pl.ds(0, plan.body)], sem.at[0])
    load_ids = pltpu.make_async_copy(ids, ids_row, sem.at[1])
    load_ids.start()
    load.start()
    load_ids.wait()
    n = plan.slots
    row = jnp.broadcast_to(ids_row[...], (n, n))
    col = row.astype(jnp.float32).T.astype(jnp.int32)
    here, there = (lax.broadcasted_iota(jnp.int32, (n, n), i) for i in range(2))
    same = (row >> shift_of(plan.kt)) == (col >> shift_of(plan.kt))
    place_row = jnp.sum(jnp.where(same & (here < there), 1, 0), axis=0, keepdims=True)
    place_col = jnp.sum(jnp.where(same & (there < here), 1, 0), axis=1, keepdims=True)
    line = lax.broadcasted_iota(jnp.int32, (plan.head, n), 0)
    ids_line = jnp.broadcast_to(ids_row[...], (plan.head, n))
    block = ids_line >> shift_of(plan.kt)
    lane = lax.broadcasted_iota(jnp.int32, (n, plan.tile), 1)
    tile_at = lax.broadcasted_iota(jnp.int32, (n, plan.tile), 0)

    def spread(values, where):
        return lax.dot_general(
            values.astype(jnp.float32).astype(jnp.bfloat16),
            jnp.where(where, 1.0, 0.0).astype(jnp.bfloat16),
            (((1,), (0,)), ((), ())),
            preferred_element_type=jnp.float32,
        )

    missing = jnp.where(block == line, (ids_line & (plan.kt - 1)) - plan.kt, 0)
    places = spread(missing, place_col == lane) + plan.kt
    slot = jnp.where(line == plan.n_col, block * CAP + place_row, 0)
    slots = spread(slot, tile_at == lane)
    top = lax.broadcasted_iota(jnp.int32, (plan.head, plan.tile), 0)
    head = jnp.where(top == plan.n_col, slots, places)
    buf[plan.body :, :] = head.astype(jnp.bfloat16)
    load.wait()
    store = pltpu.make_async_copy(buf, packed, sem.at[0])
    store.start()
    store.wait()


def pack(plan, ids, tiles):
    ids, tiles = (pltpu.with_memory_space_constraint(x, pltpu.HBM) for x in (ids, tiles))
    return pl.pallas_call(
        functools.partial(pack_kernel, plan),
        out_shape=jax.ShapeDtypeStruct((plan.packed, plan.tile), jnp.bfloat16),
        in_specs=[HBM, HBM],
        out_specs=HBM,
        scratch_shapes=[
            pltpu.VMEM(ids.shape, jnp.int32),
            pltpu.VMEM((plan.packed, plan.tile), jnp.bfloat16),
            pltpu.SemaphoreType.DMA((2,)),
        ],
        compiler_params=pltpu.CompilerParams(vmem_limit_bytes=8 * 1024 * 1024),
        cost_estimate=cost(plan, 2 * plan.packed * plan.tile * 2),
        name="pack_tiles",
    )(ids, tiles)


def cost(plan, moved, flops=0):
    return pl.CostEstimate(flops=flops, bytes_accessed=moved, transcendentals=0)


def bucket_kernel(plan, count, *rest):
    packed, (buf, bodies, tops, heads, line, places, sem) = rest[:count], rest[count:]
    rows, piece = plan.pairs, count * plan.bucket
    loads = []
    for i, ref in enumerate(packed):
        top = tops.at[pl.ds(i * plan.head, plan.head)]
        loads.append(pltpu.make_async_copy(ref.at[pl.ds(plan.body, plan.head)], top, sem.at[2 * i]))
        loads[-1].start()
    for i, ref in enumerate(packed):
        body = bodies.at[pl.ds(i * plan.body, plan.body)]
        loads.append(pltpu.make_async_copy(ref.at[pl.ds(0, plan.body)], body, sem.at[2 * i + 1]))
        loads[-1].start()
    col = lax.axis_index("col")
    for i in range(count):
        loads[i].wait()
        head = tops[i * plan.head : (i + 1) * plan.head, :].astype(jnp.float32)
        heads[i * plan.head : (i + 1) * plan.head, :] = head
        slot = head[plan.n_col : plan.n_col + 1, :].astype(jnp.int32)
        m = (slot >> shift_of(CAP)) ^ col
        at = (m >> 1) * piece + i * plan.bucket + (slot & (CAP - 1)) * rows
        line[i : i + 1, :] = jnp.where((m & 1) == 0, at, plan.n_pair * piece)
    copy = pltpu.make_async_copy(line, places, sem.at[2 * count])
    copy.start()
    for i in range(count):
        for chip in range(plan.n_pair):
            ids = heads[pl.ds(i * plan.head + (col ^ (2 * chip)), 1), :]
            at = chip * piece + i * plan.bucket + CAP * rows
            buf[at : at + rows, :] = jnp.broadcast_to(ids, (rows, plan.tile)).astype(jnp.bfloat16)
    copy.wait()
    for i in range(count):
        loads[count + i].wait()

        def step(s, _, i=i):
            at = pl.multiple_of(places[i, s], rows)
            tile = bodies[pl.ds(pl.multiple_of(i * plan.body + s * rows, rows), rows), :]
            buf[pl.ds(at, rows), :] = tile
            return 0

        lax.fori_loop(0, plan.slots, step, 0, unroll=16)


def bucket(plan, packed):
    count = len(packed)
    piece = count * plan.bucket
    lines = -(-count // 8) * 8
    bf16 = jnp.bfloat16
    out = pl.pallas_call(
        functools.partial(bucket_kernel, plan, count),
        out_shape=pltpu.VMEM((plan.n_pair * piece + plan.pairs, plan.tile), bf16),
        in_specs=[HBM] * count,
        out_specs=VMEM,
        scratch_shapes=[
            pltpu.VMEM((count * plan.body, plan.tile), bf16),
            pltpu.VMEM((count * plan.head, plan.tile), bf16),
            pltpu.VMEM((count * plan.head, plan.tile), jnp.float32),
            pltpu.VMEM((lines, plan.tile), jnp.int32),
            pltpu.SMEM((lines, plan.tile), jnp.int32),
            pltpu.SemaphoreType.DMA((2 * count + 1,)),
        ],
        compiler_params=pltpu.CompilerParams(vmem_limit_bytes=12 * 1024 * 1024),
        cost_estimate=cost(plan, 4 * plan.n_pair * piece * plan.tile * 2),
        name="bucket_tiles",
    )(*packed)
    return [out[i * piece : (i + 1) * piece] for i in range(plan.n_pair)]


def place(plan, planes, parts, lam, tiles, line, places, sem, part_sem):
    rows = plan.pairs
    half = plan.n_pair * plan.owned
    sources, loads, at = [], [], 0
    for ref, (chips, ds) in zip(parts, planes, strict=True):
        loads.append(pltpu.make_async_copy(ref, tiles.at[pl.ds(at, ref.shape[0])], part_sem.at[len(loads)]))
        loads[-1].start()
        for chip in chips:
            for d in ds:
                for side in range(2):
                    sources.append((at, d, 2 * chip + side))
                    at += plan.bucket
    yield
    for load in loads:
        load.wait()
    for i, (base, _, _) in enumerate(sources):
        head = tiles[base + CAP * rows : base + plan.bucket, :].astype(jnp.float32)
        line[i : i + 1, :] = head[0:1, :].astype(jnp.int32)
    copy = pltpu.make_async_copy(line, places, sem)
    copy.start()
    copy.wait()
    row, col = lax.axis_index("row"), lax.axis_index("col")
    per_owner = plan.owned // rows
    for i, (base, d, m) in enumerate(sources):
        group = (row ^ d) * plan.n_col + (col ^ m)
        rel = (group >> shift_of(per_owner)) ^ col
        to = (rel & 1) * half + (rel >> 1) * plan.owned + (group & (per_owner - 1)) * rows
        for s in range(CAP):
            at = places[i, s]
            line_at = pl.multiple_of(jnp.where(at < plan.kt, to, 2 * half), rows)
            at = pl.multiple_of((at & (plan.kt - 1)) * plan.tile, plan.tile)
            tile = tiles[base + s * rows : base + (s + 1) * rows, :]
            lam[pl.ds(line_at, rows), pl.ds(at, plan.tile)] = tile
    yield


def place_scratch(plan, planes):
    count = sum(2 * len(chips) * len(ds) for chips, ds in planes)
    lines = -(-count // 8) * 8
    return [
        pltpu.VMEM((count * plan.bucket, plan.tile), jnp.bfloat16),
        pltpu.VMEM((lines, plan.tile), jnp.int32),
        pltpu.SMEM((lines, plan.tile), jnp.int32),
        pltpu.SemaphoreType.DMA,
        pltpu.SemaphoreType.DMA((len(planes),)),
    ]


def lam_shape(plan):
    return pltpu.VMEM((2 * plan.n_pair * plan.owned + plan.pairs, plan.cd), jnp.bfloat16)


def early_kernel(plan, planes, block, integrals, *rest):
    parts, (lam, staged, *scratch, stage_sem) = rest[: len(planes)], rest[len(planes) :]
    placing = place(plan, planes, parts, lam, *scratch)
    next(placing)
    copies = []
    for i in range(plan.ab // block):
        here = pl.ds(i * block, block)
        copies.append(pltpu.make_async_copy(integrals.at[here], staged.at[here], stage_sem.at[i]))
        copies[-1].start()
    lam[...] = jnp.zeros(lam.shape, lam.dtype)
    next(placing)
    for copy in copies:
        copy.wait()


def place_early(plan, planes, parts, integrals, block=256):
    integrals = pltpu.with_memory_space_constraint(integrals, pltpu.HBM)
    return pl.pallas_call(
        functools.partial(early_kernel, plan, planes, block),
        out_shape=[lam_shape(plan), pltpu.VMEM(integrals.shape, integrals.dtype)],
        in_specs=[HBM] * (1 + len(parts)),
        out_specs=[VMEM, VMEM],
        scratch_shapes=place_scratch(plan, planes) + [pltpu.SemaphoreType.DMA((plan.ab // block,))],
        compiler_params=pltpu.CompilerParams(vmem_limit_bytes=12 * 1024 * 1024),
        cost_estimate=cost(plan, 2 * plan.ab * plan.cd * 2),
        name="place_early",
    )(integrals, *parts)


def more_kernel(plan, planes, _, *rest):
    parts, (lam, *scratch) = rest[: len(planes)], rest[len(planes) :]
    placing = place(plan, planes, parts, lam, *scratch)
    next(placing)
    next(placing)


def place_more(plan, lam, planes, parts):
    return pl.pallas_call(
        functools.partial(more_kernel, plan, planes),
        out_shape=lam_shape(plan),
        in_specs=[VMEM] + [HBM] * len(parts),
        out_specs=VMEM,
        input_output_aliases={0: 0},
        scratch_shapes=place_scratch(plan, planes),
        compiler_params=pltpu.CompilerParams(vmem_limit_bytes=12 * 1024 * 1024),
        cost_estimate=cost(plan, 4 * 1024 * 1024),
        name="place_more",
    )(lam, *parts)


def send_kernel(plan, planes, block, _, cols, *rest):
    parts, (lam, send, *scratch) = rest[: len(planes)], rest[len(planes) :]
    placing = place(plan, planes, parts, lam, *scratch)
    next(placing)
    next(placing)
    multiply(plan, block, lam, plan.n_pair * plan.owned, cols, send)


def send_product(plan, lam, planes, parts, integrals, block=256):
    half = plan.n_pair * plan.owned
    return pl.pallas_call(
        functools.partial(send_kernel, plan, planes, block),
        out_shape=[lam_shape(plan), pltpu.VMEM((half, plan.ab), jnp.float32)],
        in_specs=[VMEM, VMEM] + [HBM] * len(parts),
        out_specs=[VMEM, VMEM],
        input_output_aliases={0: 0},
        scratch_shapes=place_scratch(plan, planes),
        compiler_params=pltpu.CompilerParams(vmem_limit_bytes=20 * 1024 * 1024),
        cost_estimate=cost(plan, plan.ab * plan.cd * 4, 4 * half * plan.ab * plan.cd),
        name="place_and_multiply",
    )(lam, integrals, *parts)


def multiply(plan, block, lam, first, cols, out):
    for i in range(0, plan.ab, block):
        out[:, i : i + block] = lax.dot_general(
            lam[first : first + out.shape[0], :],
            cols[i : i + block, :],
            (((1,), (1,)), ((), ())),
            preferred_element_type=jnp.float32,
        )


def keep_kernel(plan, block, lam, cols, out):
    multiply(plan, block, lam, 0, cols, out)


def keep_product(plan, lam, integrals, block=256):
    half = plan.n_pair * plan.owned
    return pl.pallas_call(
        functools.partial(keep_kernel, plan, block),
        out_shape=pltpu.VMEM((half, plan.ab), jnp.float32),
        in_specs=[VMEM, VMEM],
        out_specs=VMEM,
        compiler_params=pltpu.CompilerParams(vmem_limit_bytes=20 * 1024 * 1024),
        cost_estimate=cost(plan, (plan.ab + half) * plan.cd * 2, 2 * half * plan.ab * plan.cd),
        name="multiply_kept",
    )(lam, integrals)


def chunks_of(plan):
    return plan.ab // plan.tile


def words_shape(plan):
    return (chunks_of(plan) // 2 * plan.owned + chunks_of(plan), plan.tile)


def code_kernel(plan, keep, got, mine, *rest):
    words, square = rest[:-1], rest[-1]
    rows, tile, chunks = plan.owned, plan.tile, chunks_of(plan)
    lane = lax.broadcasted_iota(jnp.int32, (rows, tile), 1)
    mine[...] = keep[:rows, :] + got[:rows, :]
    square[...] = jnp.zeros(square.shape, jnp.float32)
    for m, out in enumerate(words, 1):
        here = slice(m * rows, (m + 1) * rows)
        cells = [slice(j * tile, (j + 1) * tile) for j in range(chunks)]
        sums = [keep[here, cell] + got[here, cell] for cell in cells]
        most = jnp.zeros((rows, tile), jnp.float32)
        for j, part in enumerate(sums):
            most = jnp.where(lane == j, jnp.max(jnp.abs(part), axis=1, keepdims=True), most)
        power = jnp.floor(jnp.log2(jnp.maximum(most, 2.0**-106)) + 1.001)
        square[:rows, :] = power
        scale = jnp.exp2(15.0 - power)
        counts = []
        for j, part in enumerate(sums):
            count = jnp.floor(part * scale[:, j : j + 1] + 0.5)
            counts.append(jnp.clip(count, -32767.0, 32767.0).astype(jnp.int32))
        for j in range(chunks // 2):
            word = (counts[j] << 16) | (counts[j + chunks // 2] & 65535)
            out[j * rows : (j + 1) * rows, :] = word
        out[chunks // 2 * rows :, :] = square[...].T[:chunks, :].astype(jnp.int32)


def code_sums(plan, keep, got):
    block = pltpu.VMEM((plan.owned, plan.ab), jnp.float32)
    return pl.pallas_call(
        functools.partial(code_kernel, plan),
        out_shape=[block] + [pltpu.VMEM(words_shape(plan), jnp.int32)] * (plan.n_pair - 1),
        in_specs=[VMEM] * 2,
        out_specs=[VMEM] * plan.n_pair,
        scratch_shapes=[pltpu.VMEM((plan.tile, plan.tile), jnp.float32)],
        compiler_params=pltpu.CompilerParams(vmem_limit_bytes=20 * 1024 * 1024),
        cost_estimate=cost(plan, 4 * plan.n_pair * plan.owned * plan.ab * 4),
        name="code_sums",
    )(keep, got)


def total_kernel(plan, mine, *rest):
    words, (out, square) = rest[:-2], rest[-2:]
    rows, tile, chunks = plan.owned, plan.tile, chunks_of(plan)
    out[...] = mine[...]
    square[...] = jnp.zeros(square.shape, jnp.float32)
    for ref in words:
        square[:chunks, :] = ref[chunks // 2 * rows :, :].astype(jnp.float32)
        scale = jnp.exp2(square[...].T[:rows, :] - 15.0)
        for j in range(chunks):
            at = j % (chunks // 2) * rows
            word = ref[at : at + rows, :]
            count = (word if j < chunks // 2 else word << 16) >> 16
            cell = slice(j * tile, (j + 1) * tile)
            out[:, cell] += count.astype(jnp.float32) * scale[:, j : j + 1]
    out[...] = 0.5 * out[...]


def total_sums(plan, mine, words):
    return pl.pallas_call(
        functools.partial(total_kernel, plan),
        out_shape=jax.ShapeDtypeStruct((plan.owned, plan.ab), jnp.float32),
        in_specs=[VMEM] * (1 + len(words)),
        out_specs=VMEM,
        scratch_shapes=[pltpu.VMEM((plan.tile, plan.tile), jnp.float32)],
        compiler_params=pltpu.CompilerParams(vmem_limit_bytes=20 * 1024 * 1024),
        cost_estimate=cost(plan, 4 * plan.n_pair * plan.owned * plan.ab * 4),
        name="total_sums",
    )(mine, *words)


def swap(x, axis, m):
    return lax.ppermute(x, axis, [(i, i ^ m) for i in range(lax.axis_size(axis))])


def shards(lam_tiles, lam_ids, integrals):
    plan = Plan(lam_tiles, integrals)
    packed = pack(plan, lam_ids, lam_tiles.reshape(plan.body, plan.tile))
    chips = range(plan.n_pair)

    def spread(ds):
        out = bucket(plan, [raw for d in ds for raw in (arrived[d], swap(arrived[d], "col", 1))])
        return [out[0]] + [swap(out[m], "col", 2 * m) for m in range(1, plan.n_pair)]

    bit = plan.n_row // 2
    arrived = {0: packed, bit: swap(packed, "row", bit)}
    own = spread([0])
    arrived[bit], own = lax.optimization_barrier((arrived[bit], own))
    while bit > 1:
        bit //= 2
        arrived.update({d | bit: swap(raw, "row", bit) for d, raw in arrived.items() if d or bit > 1})
    *middle, last = sorted(arrived)[1:]
    early = spread(middle)
    planes = [((chip,), (0,)) for chip in chips]
    lam, staged = place_early(plan, planes, own, integrals)
    arrived[last], early[1], lam, staged = lax.optimization_barrier(
        (arrived[last], early[1], lam, staged)
    )
    near = swap(jnp.concatenate(own, axis=0), "row", 1)
    late = spread([last])
    lam = place_more(plan, lam, [((chip,), tuple(middle)) for chip in chips], early)
    planes = [(chips, (1,))] + [((chip,), (last,)) for chip in chips]
    lam, send = send_product(plan, lam, planes, [near] + late, staged)
    got = swap(send, "col", 1)
    keep = keep_product(plan, lam, staged)
    mine, *words = code_sums(plan, keep, got)
    return total_sums(plan, mine, [swap(word, "col", 2 * m) for m, word in enumerate(words, 1)])


def solution(mesh):
    return jax.shard_map(
        shards,
        mesh=mesh,
        in_specs=(P(("row", "col"), None, None, None), P(("row", "col"), None), P("row", "col")),
        out_specs=P("col", "row"),
        check_vma=False,
    )
```

```python
import functools

import jax
import jax.numpy as jnp
from jax import lax
from jax.experimental import pallas as pl
from jax.experimental.pallas import tpu as pltpu
from jax.sharding import PartitionSpec as P

CAP = 16

VMEM = pl.BlockSpec(memory_space=pltpu.VMEM)
HBM = pl.BlockSpec(memory_space=pltpu.HBM)


def shift_of(size):
    assert size & (size - 1) == 0
    return size.bit_length() - 1


class Plan:
    def __init__(self, lam_tiles, integrals):
        self.n_row = lax.axis_size("row")
        self.n_col = lax.axis_size("col")
        g_dev, self.slots, self.pairs, self.tile = lam_tiles.shape
        assert g_dev == 1 and self.pairs == 16 and self.slots <= self.tile
        self.ab, self.cd = integrals.shape
        self.kt = self.cd // self.tile
        self.n_pair = self.n_col // 2
        self.per_row = self.n_col // self.n_row
        assert self.per_row % 2 == 0
        self.owned = self.n_col * self.pairs // self.per_row
        self.height = self.n_col * self.pairs
        self.bucket = (CAP + 1) * self.pairs
        self.head = -(-(self.n_col + 1) // 16) * 16
        self.body = self.slots * self.pairs
        self.packed = self.body + self.head


def pack_kernel(plan, ids, tiles, packed, ids_row, buf, sem):
    load = pltpu.make_async_copy(tiles, buf.at[pl.ds(0, plan.body)], sem.at[0])
    load_ids = pltpu.make_async_copy(ids, ids_row, sem.at[1])
    load_ids.start()
    load.start()
    load_ids.wait()
    n = plan.slots
    row = jnp.broadcast_to(ids_row[...], (n, n))
    col = row.astype(jnp.float32).T.astype(jnp.int32)
    here, there = (lax.broadcasted_iota(jnp.int32, (n, n), i) for i in range(2))
    same = (row >> shift_of(plan.kt)) == (col >> shift_of(plan.kt))
    place_row = jnp.sum(jnp.where(same & (here < there), 1, 0), axis=0, keepdims=True)
    place_col = jnp.sum(jnp.where(same & (there < here), 1, 0), axis=1, keepdims=True)
    line = lax.broadcasted_iota(jnp.int32, (plan.head, n), 0)
    ids_line = jnp.broadcast_to(ids_row[...], (plan.head, n))
    block = ids_line >> shift_of(plan.kt)
    lane = lax.broadcasted_iota(jnp.int32, (n, plan.tile), 1)
    tile_at = lax.broadcasted_iota(jnp.int32, (n, plan.tile), 0)

    def spread(values, where):
        return lax.dot_general(
            values.astype(jnp.float32).astype(jnp.bfloat16),
            jnp.where(where, 1.0, 0.0).astype(jnp.bfloat16),
            (((1,), (0,)), ((), ())),
            preferred_element_type=jnp.float32,
        )

    missing = jnp.where(block == line, (ids_line & (plan.kt - 1)) - plan.kt, 0)
    places = spread(missing, place_col == lane) + plan.kt
    slot = jnp.where(line == plan.n_col, block * CAP + place_row, 0)
    slots = spread(slot, tile_at == lane)
    top = lax.broadcasted_iota(jnp.int32, (plan.head, plan.tile), 0)
    head = jnp.where(top == plan.n_col, slots, places)
    buf[plan.body :, :] = head.astype(jnp.bfloat16)
    load.wait()
    store = pltpu.make_async_copy(buf, packed, sem.at[0])
    store.start()
    store.wait()


def pack(plan, ids, tiles):
    ids, tiles = (pltpu.with_memory_space_constraint(x, pltpu.HBM) for x in (ids, tiles))
    return pl.pallas_call(
        functools.partial(pack_kernel, plan),
        out_shape=jax.ShapeDtypeStruct((plan.packed, plan.tile), jnp.bfloat16),
        in_specs=[HBM, HBM],
        out_specs=HBM,
        scratch_shapes=[
            pltpu.VMEM(ids.shape, jnp.int32),
            pltpu.VMEM((plan.packed, plan.tile), jnp.bfloat16),
            pltpu.SemaphoreType.DMA((2,)),
        ],
        compiler_params=pltpu.CompilerParams(vmem_limit_bytes=8 * 1024 * 1024),
        cost_estimate=cost(plan, 2 * plan.packed * plan.tile * 2),
        name="pack_tiles",
    )(ids, tiles)


def cost(plan, moved, flops=0):
    return pl.CostEstimate(flops=flops, bytes_accessed=moved, transcendentals=0)


def bucket_kernel(plan, count, both, *rest):
    packed, (buf, bodies, tops, heads, line, places, sem) = rest[:count], rest[count:]
    rows, piece = plan.pairs, (2 if both else count) * plan.bucket
    loads = []
    for i, ref in enumerate(packed):
        top = tops.at[pl.ds(i * plan.head, plan.head)]
        loads.append(pltpu.make_async_copy(ref.at[pl.ds(plan.body, plan.head)], top, sem.at[2 * i]))
        loads[-1].start()
    for i, ref in enumerate(packed):
        body = bodies.at[pl.ds(i * plan.body, plan.body)]
        loads.append(pltpu.make_async_copy(ref.at[pl.ds(0, plan.body)], body, sem.at[2 * i + 1]))
        loads[-1].start()
    col = lax.axis_index("col")
    for i in range(count):
        loads[i].wait()
        head = tops[i * plan.head : (i + 1) * plan.head, :].astype(jnp.float32)
        heads[i * plan.head : (i + 1) * plan.head, :] = head
        slot = head[plan.n_col : plan.n_col + 1, :].astype(jnp.int32)
        m = (slot >> shift_of(CAP)) ^ col
        at = (m >> 1) * piece + (slot & (CAP - 1)) * rows
        if both:
            line[i : i + 1, :] = at + (m & 1) * plan.bucket
        else:
            line[i : i + 1, :] = jnp.where((m & 1) == 0, at + i * plan.bucket, plan.n_pair * piece)
    copy = pltpu.make_async_copy(line, places, sem.at[2 * count])
    copy.start()
    for i in range(2 if both else count):
        for chip in range(plan.n_pair):
            at_line = (col ^ (2 * chip + i)) if both else i * plan.head + (col ^ (2 * chip))
            ids = heads[pl.ds(at_line, 1), :]
            at = chip * piece + i * plan.bucket + CAP * rows
            buf[at : at + rows, :] = jnp.broadcast_to(ids, (rows, plan.tile)).astype(jnp.bfloat16)
    copy.wait()
    for i in range(count):
        loads[count + i].wait()

        def step(s, _, i=i):
            at = pl.multiple_of(places[i, s], rows)
            tile = bodies[pl.ds(pl.multiple_of(i * plan.body + s * rows, rows), rows), :]
            buf[pl.ds(at, rows), :] = tile
            return 0

        lax.fori_loop(0, plan.slots, step, 0, unroll=16)


def bucket(plan, packed, both=False):
    count = len(packed)
    piece = (2 if both else count) * plan.bucket
    lines = -(-count // 8) * 8
    bf16 = jnp.bfloat16
    out = pl.pallas_call(
        functools.partial(bucket_kernel, plan, count, both),
        out_shape=pltpu.VMEM((plan.n_pair * piece + plan.pairs, plan.tile), bf16),
        in_specs=[HBM] * count,
        out_specs=VMEM,
        scratch_shapes=[
            pltpu.VMEM((count * plan.body, plan.tile), bf16),
            pltpu.VMEM((count * plan.head, plan.tile), bf16),
            pltpu.VMEM((count * plan.head, plan.tile), jnp.float32),
            pltpu.VMEM((lines, plan.tile), jnp.int32),
            pltpu.SMEM((lines, plan.tile), jnp.int32),
            pltpu.SemaphoreType.DMA((2 * count + 1,)),
        ],
        compiler_params=pltpu.CompilerParams(vmem_limit_bytes=12 * 1024 * 1024),
        cost_estimate=cost(plan, 4 * plan.n_pair * piece * plan.tile * 2),
        name="bucket_tiles",
    )(*packed)
    return [out[i * piece : (i + 1) * piece] for i in range(plan.n_pair)]


def place(plan, planes, parts, lam, tiles, line, places, sem, part_sem):
    rows = plan.pairs
    half = plan.n_pair * plan.owned
    sources, loads, at = [], [], 0
    for ref, (chips, ds, *sides) in zip(parts, planes, strict=True):
        sides = sides or (0, 1)
        size = len(chips) * len(ds) * len(sides) * plan.bucket
        here = tiles.at[pl.ds(at, size)]
        loads.append(pltpu.make_async_copy(ref.at[pl.ds(0, size)], here, part_sem.at[len(loads)]))
        loads[-1].start()
        for chip in chips:
            for d in ds:
                for side in sides:
                    sources.append((at, d, 2 * chip + side))
                    at += plan.bucket
    yield
    for load in loads:
        load.wait()
    for i, (base, _, _) in enumerate(sources):
        head = tiles[base + CAP * rows : base + plan.bucket, :].astype(jnp.float32)
        line[i : i + 1, :] = head[0:1, :].astype(jnp.int32)
    copy = pltpu.make_async_copy(line, places, sem)
    copy.start()
    copy.wait()
    row, col = lax.axis_index("row"), lax.axis_index("col")
    per_owner = plan.owned // rows
    for i, (base, d, m) in enumerate(sources):
        group = (row ^ d) * plan.n_col + (col ^ m)
        rel = (group >> shift_of(per_owner)) ^ col
        to = (rel & 1) * half + (rel >> 1) * plan.owned + (group & (per_owner - 1)) * rows
        for s in range(CAP):
            at = places[i, s]
            line_at = pl.multiple_of(jnp.where(at < plan.kt, to, 2 * half), rows)
            at = pl.multiple_of((at & (plan.kt - 1)) * plan.tile, plan.tile)
            tile = tiles[base + s * rows : base + (s + 1) * rows, :]
            lam[pl.ds(line_at, rows), pl.ds(at, plan.tile)] = tile
    yield


def place_scratch(plan, planes):
    count = sum(len(chips) * len(ds) * len(sides or (0, 1)) for chips, ds, *sides in planes)
    lines = -(-count // 8) * 8
    return [
        pltpu.VMEM((count * plan.bucket, plan.tile), jnp.bfloat16),
        pltpu.VMEM((lines, plan.tile), jnp.int32),
        pltpu.SMEM((lines, plan.tile), jnp.int32),
        pltpu.SemaphoreType.DMA,
        pltpu.SemaphoreType.DMA((len(planes),)),
    ]


def lam_shape(plan):
    return pltpu.VMEM((2 * plan.n_pair * plan.owned + plan.pairs, plan.cd), jnp.bfloat16)


def stage_kernel(plan, block, integrals, staged, sem):
    copies = []
    for i in range(plan.ab // block):
        here = pl.ds(i * block, block)
        copies.append(pltpu.make_async_copy(integrals.at[here], staged.at[here], sem.at[i]))
        copies[-1].start()
    for copy in copies:
        copy.wait()


def stage(plan, integrals, block=256):
    integrals = pltpu.with_memory_space_constraint(integrals, pltpu.HBM)
    return pl.pallas_call(
        functools.partial(stage_kernel, plan, block),
        out_shape=pltpu.VMEM(integrals.shape, integrals.dtype),
        in_specs=[HBM],
        out_specs=VMEM,
        scratch_shapes=[pltpu.SemaphoreType.DMA((plan.ab // block,))],
        compiler_params=pltpu.CompilerParams(vmem_limit_bytes=2 * 1024 * 1024),
        cost_estimate=cost(plan, 2 * plan.ab * plan.cd * 2),
        name="stage_integrals",
    )(integrals)


def early_kernel(plan, planes, *rest):
    parts, (lam, *scratch) = rest[: len(planes)], rest[len(planes) :]
    placing = place(plan, planes, parts, lam, *scratch)
    next(placing)
    lam[...] = jnp.zeros(lam.shape, lam.dtype)
    next(placing)


def place_early(plan, planes, parts):
    return pl.pallas_call(
        functools.partial(early_kernel, plan, planes),
        out_shape=lam_shape(plan),
        in_specs=[HBM] * len(parts),
        out_specs=VMEM,
        scratch_shapes=place_scratch(plan, planes),
        compiler_params=pltpu.CompilerParams(vmem_limit_bytes=12 * 1024 * 1024),
        cost_estimate=cost(plan, 4 * 1024 * 1024),
        name="place_early",
    )(*parts)


def more_kernel(plan, planes, _, *rest):
    parts, (lam, *scratch) = rest[: len(planes)], rest[len(planes) :]
    placing = place(plan, planes, parts, lam, *scratch)
    next(placing)
    next(placing)


def place_more(plan, lam, planes, parts):
    return pl.pallas_call(
        functools.partial(more_kernel, plan, planes),
        out_shape=lam_shape(plan),
        in_specs=[VMEM] + [HBM] * len(parts),
        out_specs=VMEM,
        input_output_aliases={0: 0},
        scratch_shapes=place_scratch(plan, planes),
        compiler_params=pltpu.CompilerParams(vmem_limit_bytes=12 * 1024 * 1024),
        cost_estimate=cost(plan, 4 * 1024 * 1024),
        name="place_more",
    )(lam, *parts)


def send_kernel(plan, planes, block, _, cols, *rest):
    parts, (lam, send, *scratch) = rest[: len(planes)], rest[len(planes) :]
    placing = place(plan, planes, parts, lam, *scratch)
    next(placing)
    next(placing)
    multiply(plan, block, lam, plan.n_pair * plan.owned, cols, send)


def send_product(plan, lam, planes, parts, integrals, block=256):
    half = plan.n_pair * plan.owned
    return pl.pallas_call(
        functools.partial(send_kernel, plan, planes, block),
        out_shape=[lam_shape(plan), pltpu.VMEM((half, plan.ab), jnp.float32)],
        in_specs=[VMEM, VMEM] + [HBM] * len(parts),
        out_specs=[VMEM, VMEM],
        input_output_aliases={0: 0},
        scratch_shapes=place_scratch(plan, planes),
        compiler_params=pltpu.CompilerParams(vmem_limit_bytes=20 * 1024 * 1024),
        cost_estimate=cost(plan, plan.ab * plan.cd * 4, 4 * half * plan.ab * plan.cd),
        name="place_and_multiply",
    )(lam, integrals, *parts)


def multiply(plan, block, lam, first, cols, out):
    for i in range(0, plan.ab, block):
        out[:, i : i + block] = lax.dot_general(
            lam[first : first + out.shape[0], :],
            cols[i : i + block, :],
            (((1,), (1,)), ((), ())),
            preferred_element_type=jnp.float32,
        )


def keep_kernel(plan, block, lam, cols, out):
    multiply(plan, block, lam, 0, cols, out)


def keep_product(plan, lam, integrals, block=256):
    half = plan.n_pair * plan.owned
    return pl.pallas_call(
        functools.partial(keep_kernel, plan, block),
        out_shape=pltpu.VMEM((half, plan.ab), jnp.float32),
        in_specs=[VMEM, VMEM],
        out_specs=VMEM,
        compiler_params=pltpu.CompilerParams(vmem_limit_bytes=20 * 1024 * 1024),
        cost_estimate=cost(plan, (plan.ab + half) * plan.cd * 2, 2 * half * plan.ab * plan.cd),
        name="multiply_kept",
    )(lam, integrals)


def chunks_of(plan):
    return plan.ab // plan.tile


def words_shape(plan):
    return (chunks_of(plan) // 2 * plan.owned + chunks_of(plan), plan.tile)


def code_kernel(plan, keep, got, mine, *rest):
    words, square = rest[:-1], rest[-1]
    rows, tile, chunks = plan.owned, plan.tile, chunks_of(plan)
    lane = lax.broadcasted_iota(jnp.int32, (rows, tile), 1)
    mine[...] = keep[:rows, :] + got[:rows, :]
    square[...] = jnp.zeros(square.shape, jnp.float32)
    for m, out in enumerate(words, 1):
        here = slice(m * rows, (m + 1) * rows)
        cells = [slice(j * tile, (j + 1) * tile) for j in range(chunks)]
        sums = [keep[here, cell] + got[here, cell] for cell in cells]
        most = jnp.zeros((rows, tile), jnp.float32)
        for j, part in enumerate(sums):
            most = jnp.where(lane == j, jnp.max(jnp.abs(part), axis=1, keepdims=True), most)
        power = jnp.floor(jnp.log2(jnp.maximum(most, 2.0**-106)) + 1.001)
        square[:rows, :] = power
        scale = jnp.exp2(15.0 - power)
        counts = []
        for j, part in enumerate(sums):
            count = jnp.floor(part * scale[:, j : j + 1] + 0.5)
            counts.append(jnp.clip(count, -32767.0, 32767.0).astype(jnp.int32))
        for j in range(chunks // 2):
            word = (counts[j] << 16) | (counts[j + chunks // 2] & 65535)
            out[j * rows : (j + 1) * rows, :] = word
        out[chunks // 2 * rows :, :] = square[...].T[:chunks, :].astype(jnp.int32)


def code_sums(plan, keep, got):
    block = pltpu.VMEM((plan.owned, plan.ab), jnp.float32)
    return pl.pallas_call(
        functools.partial(code_kernel, plan),
        out_shape=[block] + [pltpu.VMEM(words_shape(plan), jnp.int32)] * (plan.n_pair - 1),
        in_specs=[VMEM] * 2,
        out_specs=[VMEM] * plan.n_pair,
        scratch_shapes=[pltpu.VMEM((plan.tile, plan.tile), jnp.float32)],
        compiler_params=pltpu.CompilerParams(vmem_limit_bytes=20 * 1024 * 1024),
        cost_estimate=cost(plan, 4 * plan.n_pair * plan.owned * plan.ab * 4),
        name="code_sums",
    )(keep, got)


def total_kernel(plan, mine, *rest):
    words, (out, sums, square, sem) = rest[:-4], rest[-4:]
    rows, tile, chunks = plan.owned, plan.tile, chunks_of(plan)
    square[...] = jnp.zeros(square.shape, jnp.float32)
    scales = []
    for ref in words:
        square[:chunks, :] = ref[chunks // 2 * rows :, :].astype(jnp.float32)
        scales.append(jnp.exp2(square[...].T[:rows, :] - 16.0))
    copies = []
    for j in range(chunks):
        cell = slice(j * tile, (j + 1) * tile)
        at = j % (chunks // 2) * rows
        total = 0.5 * mine[:, cell]
        for ref, scale in zip(words, scales, strict=True):
            word = ref[at : at + rows, :]
            count = (word if j < chunks // 2 else word << 16) >> 16
            total += count.astype(jnp.float32) * scale[:, j : j + 1]
        sums[:, cell] = total
        copies.append(pltpu.make_async_copy(sums.at[:, cell], out.at[:, cell], sem.at[j]))
        copies[-1].start()
    for copy in copies:
        copy.wait()


def total_sums(plan, mine, words):
    return pl.pallas_call(
        functools.partial(total_kernel, plan),
        out_shape=jax.ShapeDtypeStruct((plan.owned, plan.ab), jnp.float32),
        in_specs=[VMEM] * (1 + len(words)),
        out_specs=HBM,
        scratch_shapes=[
            pltpu.VMEM((plan.owned, plan.ab), jnp.float32),
            pltpu.VMEM((plan.tile, plan.tile), jnp.float32),
            pltpu.SemaphoreType.DMA((chunks_of(plan),)),
        ],
        compiler_params=pltpu.CompilerParams(vmem_limit_bytes=20 * 1024 * 1024),
        cost_estimate=cost(plan, 4 * plan.n_pair * plan.owned * plan.ab * 4),
        name="total_sums",
    )(mine, *words)


def swap(x, axis, m):
    return lax.ppermute(x, axis, [(i, i ^ m) for i in range(lax.axis_size(axis))])


def shards(lam_tiles, lam_ids, integrals):
    plan = Plan(lam_tiles, integrals)
    packed = pack(plan, lam_ids, lam_tiles.reshape(plan.body, plan.tile))
    chips = range(plan.n_pair)

    def spread(ds):
        out = bucket(plan, [raw for d in ds for raw in (arrived[d], swap(arrived[d], "col", 1))])
        return [out[0]] + [swap(out[m], "col", 2 * m) for m in range(1, plan.n_pair)]

    bit = plan.n_row // 2
    arrived = {0: packed, bit: swap(packed, "row", bit)}
    own = spread([0])
    staged = stage(plan, integrals)
    arrived[bit], own, staged = lax.optimization_barrier((arrived[bit], own, staged))
    while bit > 1:
        bit //= 2
        arrived.update({d | bit: swap(raw, "row", bit) for d, raw in arrived.items() if d or bit > 1})
    *middle, last = sorted(arrived)[1:]
    early = spread(middle)
    arrived[last], early[1] = lax.optimization_barrier((arrived[last], early[1]))
    near = swap(jnp.concatenate(own, axis=0), "row", 1)
    late = bucket(plan, [arrived[last]], both=True)
    late = [late[0]] + [swap(late[m], "col", 2 * m) for m in range(1, plan.n_pair)]
    lam = place_early(plan, [((chip,), (0,)) for chip in chips], own)
    lam = place_more(plan, lam, [((chip,), tuple(middle)) for chip in chips], early)
    late, lam, near = lax.optimization_barrier((late, lam, near))
    cross = swap(jnp.concatenate([part[plan.bucket :] for part in late], axis=0), "col", 1)
    lam = place_more(plan, lam, [(chips, (1,))], [near])
    planes = [((chip,), (last,), 0) for chip in chips] + [(chips, (last,), 1)]
    lam, send = send_product(plan, lam, planes, late + [cross], staged)
    got = swap(send, "col", 1)
    keep = keep_product(plan, lam, staged)
    mine, *words = code_sums(plan, keep, got)
    return total_sums(plan, mine, [swap(word, "col", 2 * m) for m, word in enumerate(words, 1)])


def solution(mesh):
    return jax.shard_map(
        shards,
        mesh=mesh,
        in_specs=(P(("row", "col"), None, None, None), P(("row", "col"), None), P("row", "col")),
        out_specs=P("col", "row"),
        check_vma=False,
    )
```

```python
import functools

import jax
import jax.numpy as jnp
from jax import lax
from jax.experimental import pallas as pl
from jax.experimental.pallas import tpu as pltpu
from jax.sharding import PartitionSpec as P

CAP = 16

VMEM = pl.BlockSpec(memory_space=pltpu.VMEM)
HBM = pl.BlockSpec(memory_space=pltpu.HBM)


def shift_of(size):
    assert size & (size - 1) == 0
    return size.bit_length() - 1


class Plan:
    def __init__(self, lam_tiles, integrals):
        self.n_row = lax.axis_size("row")
        self.n_col = lax.axis_size("col")
        g_dev, self.slots, self.pairs, self.tile = lam_tiles.shape
        assert g_dev == 1 and self.pairs == 16 and self.slots <= self.tile
        self.ab, self.cd = integrals.shape
        self.kt = self.cd // self.tile
        self.n_pair = self.n_col // 2
        self.per_row = self.n_col // self.n_row
        assert self.per_row % 2 == 0
        self.owned = self.n_col * self.pairs // self.per_row
        self.height = self.n_col * self.pairs
        self.bucket = (CAP + 1) * self.pairs
        self.head = -(-(self.n_col + 1) // 16) * 16
        self.body = self.slots * self.pairs
        self.packed = self.body + self.head


def pack_kernel(plan, ids, tiles, packed, ids_row, sem):
    load = pltpu.make_async_copy(tiles, packed.at[pl.ds(0, plan.body)], sem.at[0])
    load_ids = pltpu.make_async_copy(ids, ids_row, sem.at[1])
    load_ids.start()
    load.start()
    load_ids.wait()
    n = plan.slots
    row = jnp.broadcast_to(ids_row[...], (n, n))
    col = row.astype(jnp.float32).T.astype(jnp.int32)
    here, there = (lax.broadcasted_iota(jnp.int32, (n, n), i) for i in range(2))
    same = (row >> shift_of(plan.kt)) == (col >> shift_of(plan.kt))
    place_row = jnp.sum(jnp.where(same & (here < there), 1, 0), axis=0, keepdims=True)
    place_col = jnp.sum(jnp.where(same & (there < here), 1, 0), axis=1, keepdims=True)
    line = lax.broadcasted_iota(jnp.int32, (plan.head, n), 0)
    ids_line = jnp.broadcast_to(ids_row[...], (plan.head, n))
    block = ids_line >> shift_of(plan.kt)
    lane = lax.broadcasted_iota(jnp.int32, (n, plan.tile), 1)
    tile_at = lax.broadcasted_iota(jnp.int32, (n, plan.tile), 0)

    def spread(values, where):
        return lax.dot_general(
            values.astype(jnp.float32).astype(jnp.bfloat16),
            jnp.where(where, 1.0, 0.0).astype(jnp.bfloat16),
            (((1,), (0,)), ((), ())),
            preferred_element_type=jnp.float32,
        )

    missing = jnp.where(block == line, (ids_line & (plan.kt - 1)) - plan.kt, 0)
    places = spread(missing, place_col == lane) + plan.kt
    slot = jnp.where(line == plan.n_col, block * CAP + place_row, 0)
    slots = spread(slot, tile_at == lane)
    top = lax.broadcasted_iota(jnp.int32, (plan.head, plan.tile), 0)
    head = jnp.where(top == plan.n_col, slots, places)
    packed[plan.body :, :] = head.astype(jnp.bfloat16)
    load.wait()


def pack(plan, ids, tiles):
    ids, tiles = (pltpu.with_memory_space_constraint(x, pltpu.HBM) for x in (ids, tiles))
    return pl.pallas_call(
        functools.partial(pack_kernel, plan),
        out_shape=pltpu.VMEM((plan.packed, plan.tile), jnp.bfloat16),
        in_specs=[HBM, HBM],
        out_specs=VMEM,
        scratch_shapes=[
            pltpu.VMEM(ids.shape, jnp.int32),
            pltpu.SemaphoreType.DMA((2,)),
        ],
        compiler_params=pltpu.CompilerParams(vmem_limit_bytes=8 * 1024 * 1024),
        cost_estimate=cost(plan, 2 * plan.packed * plan.tile * 2),
        name="pack_tiles",
    )(ids, tiles)


def cost(plan, moved, flops=0):
    return pl.CostEstimate(flops=flops, bytes_accessed=moved, transcendentals=0)


def bucket_kernel(plan, count, both, *rest):
    packed, (buf, bodies, tops, heads, line, places, sem) = rest[:count], rest[count:]
    rows, piece = plan.pairs, (2 if both else count) * plan.bucket
    loads = []
    for i, ref in enumerate(packed):
        top = tops.at[pl.ds(i * plan.head, plan.head)]
        loads.append(pltpu.make_async_copy(ref.at[pl.ds(plan.body, plan.head)], top, sem.at[2 * i]))
        loads[-1].start()
    for i, ref in enumerate(packed):
        body = bodies.at[pl.ds(i * plan.body, plan.body)]
        loads.append(pltpu.make_async_copy(ref.at[pl.ds(0, plan.body)], body, sem.at[2 * i + 1]))
        loads[-1].start()
    col = lax.axis_index("col")
    for i in range(count):
        loads[i].wait()
        head = tops[i * plan.head : (i + 1) * plan.head, :].astype(jnp.float32)
        heads[i * plan.head : (i + 1) * plan.head, :] = head
        slot = head[plan.n_col : plan.n_col + 1, :].astype(jnp.int32)
        m = (slot >> shift_of(CAP)) ^ col
        at = (m >> 1) * piece + (slot & (CAP - 1)) * rows
        if both:
            line[i : i + 1, :] = at + (m & 1) * plan.bucket
        else:
            line[i : i + 1, :] = jnp.where((m & 1) == 0, at + i * plan.bucket, plan.n_pair * piece)
    copy = pltpu.make_async_copy(line, places, sem.at[2 * count])
    copy.start()
    for i in range(2 if both else count):
        for chip in range(plan.n_pair):
            at_line = (col ^ (2 * chip + i)) if both else i * plan.head + (col ^ (2 * chip))
            ids = heads[pl.ds(at_line, 1), :]
            at = chip * piece + i * plan.bucket + CAP * rows
            buf[at : at + rows, :] = jnp.broadcast_to(ids, (rows, plan.tile)).astype(jnp.bfloat16)
    copy.wait()
    for i in range(count):
        loads[count + i].wait()

        def step(s, _, i=i):
            at = pl.multiple_of(places[i, s], rows)
            tile = bodies[pl.ds(pl.multiple_of(i * plan.body + s * rows, rows), rows), :]
            buf[pl.ds(at, rows), :] = tile
            return 0

        lax.fori_loop(0, plan.slots, step, 0, unroll=16)


def bucket(plan, packed, both=False):
    count = len(packed)
    piece = (2 if both else count) * plan.bucket
    lines = -(-count // 8) * 8
    bf16 = jnp.bfloat16
    out = pl.pallas_call(
        functools.partial(bucket_kernel, plan, count, both),
        out_shape=pltpu.VMEM((plan.n_pair * piece + plan.pairs, plan.tile), bf16),
        in_specs=[HBM] * count,
        out_specs=VMEM,
        scratch_shapes=[
            pltpu.VMEM((count * plan.body, plan.tile), bf16),
            pltpu.VMEM((count * plan.head, plan.tile), bf16),
            pltpu.VMEM((count * plan.head, plan.tile), jnp.float32),
            pltpu.VMEM((lines, plan.tile), jnp.int32),
            pltpu.SMEM((lines, plan.tile), jnp.int32),
            pltpu.SemaphoreType.DMA((2 * count + 1,)),
        ],
        compiler_params=pltpu.CompilerParams(vmem_limit_bytes=12 * 1024 * 1024),
        cost_estimate=cost(plan, 4 * plan.n_pair * piece * plan.tile * 2),
        name="bucket_tiles",
    )(*packed)
    return [out[i * piece : (i + 1) * piece] for i in range(plan.n_pair)]


def place(plan, planes, parts, lam, tiles, line, places, sem, part_sem):
    rows = plan.pairs
    half = plan.n_pair * plan.owned
    sources, loads, at = [], [], 0
    for ref, (chips, ds, *sides) in zip(parts, planes, strict=True):
        sides = sides or (0, 1)
        size = len(chips) * len(ds) * len(sides) * plan.bucket
        here = tiles.at[pl.ds(at, size)]
        loads.append(pltpu.make_async_copy(ref.at[pl.ds(0, size)], here, part_sem.at[len(loads)]))
        loads[-1].start()
        for chip in chips:
            for d in ds:
                for side in sides:
                    sources.append((at, d, 2 * chip + side))
                    at += plan.bucket
    yield
    for load in loads:
        load.wait()
    for i, (base, _, _) in enumerate(sources):
        head = tiles[base + CAP * rows : base + plan.bucket, :].astype(jnp.float32)
        line[i : i + 1, :] = head[0:1, :].astype(jnp.int32)
    copy = pltpu.make_async_copy(line, places, sem)
    copy.start()
    copy.wait()
    row, col = lax.axis_index("row"), lax.axis_index("col")
    per_owner = plan.owned // rows
    for i, (base, d, m) in enumerate(sources):
        group = (row ^ d) * plan.n_col + (col ^ m)
        rel = (group >> shift_of(per_owner)) ^ col
        to = (rel & 1) * half + (rel >> 1) * plan.owned + (group & (per_owner - 1)) * rows
        for s in range(CAP):
            at = places[i, s]
            line_at = pl.multiple_of(jnp.where(at < plan.kt, to, 2 * half), rows)
            at = pl.multiple_of((at & (plan.kt - 1)) * plan.tile, plan.tile)
            tile = tiles[base + s * rows : base + (s + 1) * rows, :]
            lam[pl.ds(line_at, rows), pl.ds(at, plan.tile)] = tile
    yield


def place_scratch(plan, planes):
    count = sum(len(chips) * len(ds) * len(sides or (0, 1)) for chips, ds, *sides in planes)
    lines = -(-count // 8) * 8
    return [
        pltpu.VMEM((count * plan.bucket, plan.tile), jnp.bfloat16),
        pltpu.VMEM((lines, plan.tile), jnp.int32),
        pltpu.SMEM((lines, plan.tile), jnp.int32),
        pltpu.SemaphoreType.DMA,
        pltpu.SemaphoreType.DMA((len(planes),)),
    ]


def lam_shape(plan):
    return pltpu.VMEM((2 * plan.n_pair * plan.owned + plan.pairs, plan.cd), jnp.bfloat16)


def stage_kernel(plan, block, integrals, staged, sem):
    copies = []
    for i in range(plan.ab // block):
        here = pl.ds(i * block, block)
        copies.append(pltpu.make_async_copy(integrals.at[here], staged.at[here], sem.at[i]))
        copies[-1].start()
    for copy in copies:
        copy.wait()


def stage(plan, integrals, block=256):
    integrals = pltpu.with_memory_space_constraint(integrals, pltpu.HBM)
    return pl.pallas_call(
        functools.partial(stage_kernel, plan, block),
        out_shape=pltpu.VMEM(integrals.shape, integrals.dtype),
        in_specs=[HBM],
        out_specs=VMEM,
        scratch_shapes=[pltpu.SemaphoreType.DMA((plan.ab // block,))],
        compiler_params=pltpu.CompilerParams(vmem_limit_bytes=2 * 1024 * 1024),
        cost_estimate=cost(plan, 2 * plan.ab * plan.cd * 2),
        name="stage_integrals",
    )(integrals)


def early_kernel(plan, planes, *rest):
    parts, (lam, *scratch) = rest[: len(planes)], rest[len(planes) :]
    placing = place(plan, planes, parts, lam, *scratch)
    next(placing)
    lam[...] = jnp.zeros(lam.shape, lam.dtype)
    next(placing)


def place_early(plan, planes, parts):
    return pl.pallas_call(
        functools.partial(early_kernel, plan, planes),
        out_shape=lam_shape(plan),
        in_specs=[HBM] * len(parts),
        out_specs=VMEM,
        scratch_shapes=place_scratch(plan, planes),
        compiler_params=pltpu.CompilerParams(vmem_limit_bytes=12 * 1024 * 1024),
        cost_estimate=cost(plan, 4 * 1024 * 1024),
        name="place_early",
    )(*parts)


def more_kernel(plan, planes, _, *rest):
    parts, (lam, *scratch) = rest[: len(planes)], rest[len(planes) :]
    placing = place(plan, planes, parts, lam, *scratch)
    next(placing)
    next(placing)


def place_more(plan, lam, planes, parts):
    return pl.pallas_call(
        functools.partial(more_kernel, plan, planes),
        out_shape=lam_shape(plan),
        in_specs=[VMEM] + [HBM] * len(parts),
        out_specs=VMEM,
        input_output_aliases={0: 0},
        scratch_shapes=place_scratch(plan, planes),
        compiler_params=pltpu.CompilerParams(vmem_limit_bytes=12 * 1024 * 1024),
        cost_estimate=cost(plan, 4 * 1024 * 1024),
        name="place_more",
    )(lam, *parts)


def send_kernel(plan, planes, block, _, cols, *rest):
    parts, (lam, send, *scratch) = rest[: len(planes)], rest[len(planes) :]
    placing = place(plan, planes, parts, lam, *scratch)
    next(placing)
    next(placing)
    multiply(plan, block, lam, plan.n_pair * plan.owned, cols, send)


def send_product(plan, lam, planes, parts, integrals, block=256):
    half = plan.n_pair * plan.owned
    return pl.pallas_call(
        functools.partial(send_kernel, plan, planes, block),
        out_shape=[lam_shape(plan), pltpu.VMEM((half, plan.ab), jnp.float32)],
        in_specs=[VMEM, VMEM] + [HBM] * len(parts),
        out_specs=[VMEM, VMEM],
        input_output_aliases={0: 0},
        scratch_shapes=place_scratch(plan, planes),
        compiler_params=pltpu.CompilerParams(vmem_limit_bytes=20 * 1024 * 1024),
        cost_estimate=cost(plan, plan.ab * plan.cd * 4, 4 * half * plan.ab * plan.cd),
        name="place_and_multiply",
    )(lam, integrals, *parts)


def multiply(plan, block, lam, first, cols, out):
    for i in range(0, plan.ab, block):
        out[:, i : i + block] = lax.dot_general(
            lam[first : first + out.shape[0], :],
            cols[i : i + block, :],
            (((1,), (1,)), ((), ())),
            preferred_element_type=jnp.float32,
        )


def keep_kernel(plan, block, lam, cols, out):
    multiply(plan, block, lam, 0, cols, out)


def keep_product(plan, lam, integrals, block=256):
    half = plan.n_pair * plan.owned
    return pl.pallas_call(
        functools.partial(keep_kernel, plan, block),
        out_shape=pltpu.VMEM((half, plan.ab), jnp.float32),
        in_specs=[VMEM, VMEM],
        out_specs=VMEM,
        compiler_params=pltpu.CompilerParams(vmem_limit_bytes=20 * 1024 * 1024),
        cost_estimate=cost(plan, (plan.ab + half) * plan.cd * 2, 2 * half * plan.ab * plan.cd),
        name="multiply_kept",
    )(lam, integrals)


def chunks_of(plan):
    return plan.ab // plan.tile


def words_shape(plan):
    return (chunks_of(plan) // 2 * plan.owned + chunks_of(plan), plan.tile)


def code_kernel(plan, parts, keep, got, *rest):
    *words, square = rest
    rows, tile, chunks = plan.owned, plan.tile, chunks_of(plan)
    lane = lax.broadcasted_iota(jnp.int32, (rows, tile), 1)
    square[...] = jnp.zeros(square.shape, jnp.float32)
    for m, out in zip(parts, words, strict=True):
        here = slice(m * rows, (m + 1) * rows)
        if not m:
            out[...] = keep[here, :] + got[here, :]
            continue
        cells = [slice(j * tile, (j + 1) * tile) for j in range(chunks)]
        sums = [keep[here, cell] + got[here, cell] for cell in cells]
        most = jnp.zeros((rows, tile), jnp.float32)
        for j, part in enumerate(sums):
            most = jnp.where(lane == j, jnp.max(jnp.abs(part), axis=1, keepdims=True), most)
        power = jnp.floor(jnp.log2(jnp.maximum(most, 2.0**-106)) + 1.001)
        square[:rows, :] = power
        scale = jnp.exp2(15.0 - power)
        counts = []
        for j, part in enumerate(sums):
            count = jnp.floor(part * scale[:, j : j + 1] + 0.5)
            counts.append(jnp.clip(count, -32767.0, 32767.0).astype(jnp.int32))
        for j in range(chunks // 2):
            word = (counts[j] << 16) | (counts[j + chunks // 2] & 65535)
            out[j * rows : (j + 1) * rows, :] = word
        out[chunks // 2 * rows :, :] = square[...].T[:chunks, :].astype(jnp.int32)


def code_sums(plan, parts, keep, got):
    block = pltpu.VMEM((plan.owned, plan.ab), jnp.float32)
    coded = pltpu.VMEM(words_shape(plan), jnp.int32)
    return pl.pallas_call(
        functools.partial(code_kernel, plan, parts),
        out_shape=[coded if m else block for m in parts],
        in_specs=[VMEM] * 2,
        out_specs=[VMEM] * len(parts),
        scratch_shapes=[pltpu.VMEM((plan.tile, plan.tile), jnp.float32)],
        compiler_params=pltpu.CompilerParams(vmem_limit_bytes=20 * 1024 * 1024),
        cost_estimate=cost(plan, 4 * plan.n_pair * plan.owned * plan.ab * 4),
        name="code_sums",
    )(keep, got)


def total_kernel(plan, mine, *rest):
    words, (out, sums, square, sem) = rest[:-4], rest[-4:]
    rows, tile, chunks = plan.owned, plan.tile, chunks_of(plan)
    square[...] = jnp.zeros(square.shape, jnp.float32)
    scales = []
    for ref in words:
        square[:chunks, :] = ref[chunks // 2 * rows :, :].astype(jnp.float32)
        scales.append(jnp.exp2(square[...].T[:rows, :] - 16.0))
    copies = []
    for j in range(chunks):
        cell = slice(j * tile, (j + 1) * tile)
        at = j % (chunks // 2) * rows
        total = 0.5 * mine[:, cell]
        for ref, scale in zip(words, scales, strict=True):
            word = ref[at : at + rows, :]
            count = (word if j < chunks // 2 else word << 16) >> 16
            total += count.astype(jnp.float32) * scale[:, j : j + 1]
        sums[:, cell] = total
        copies.append(pltpu.make_async_copy(sums.at[:, cell], out.at[:, cell], sem.at[j]))
        copies[-1].start()
    for copy in copies:
        copy.wait()


def total_sums(plan, mine, words):
    return pl.pallas_call(
        functools.partial(total_kernel, plan),
        out_shape=jax.ShapeDtypeStruct((plan.owned, plan.ab), jnp.float32),
        in_specs=[VMEM] * (1 + len(words)),
        out_specs=HBM,
        scratch_shapes=[
            pltpu.VMEM((plan.owned, plan.ab), jnp.float32),
            pltpu.VMEM((plan.tile, plan.tile), jnp.float32),
            pltpu.SemaphoreType.DMA((chunks_of(plan),)),
        ],
        compiler_params=pltpu.CompilerParams(vmem_limit_bytes=20 * 1024 * 1024),
        cost_estimate=cost(plan, 4 * plan.n_pair * plan.owned * plan.ab * 4),
        name="total_sums",
    )(mine, *words)


def swap(x, axis, m):
    return lax.ppermute(x, axis, [(i, i ^ m) for i in range(lax.axis_size(axis))])


def shards(lam_tiles, lam_ids, integrals):
    plan = Plan(lam_tiles, integrals)
    packed = pack(plan, lam_ids, lam_tiles.reshape(plan.body, plan.tile))
    chips = range(plan.n_pair)

    def spread(ds):
        out = bucket(plan, [raw for d in ds for raw in (arrived[d], swap(arrived[d], "col", 1))])
        return [out[0]] + [swap(out[m], "col", 2 * m) for m in range(1, plan.n_pair)]

    bit = plan.n_row // 2
    arrived = {0: packed, bit: swap(packed, "row", bit)}
    own = spread([0])
    staged = stage(plan, integrals)
    arrived[bit], own, staged = lax.optimization_barrier((arrived[bit], own, staged))
    while bit > 1:
        bit //= 2
        arrived.update({d | bit: swap(raw, "row", bit) for d, raw in arrived.items() if d or bit > 1})
    *middle, last = sorted(arrived)[1:]
    early = spread(middle)
    arrived[last], early[1] = lax.optimization_barrier((arrived[last], early[1]))
    near = swap(jnp.concatenate(own, axis=0), "row", 1)
    late = bucket(plan, [arrived[last]], both=True)
    late = [late[0]] + [swap(late[m], "col", 2 * m) for m in range(1, plan.n_pair)]
    lam = place_early(plan, [((chip,), (0,)) for chip in chips], own)
    lam = place_more(plan, lam, [((chip,), tuple(middle)) for chip in chips], early)
    late, lam, near = lax.optimization_barrier((late, lam, near))
    cross = swap(jnp.concatenate([part[plan.bucket :] for part in late], axis=0), "col", 1)
    planes = [(chips, (1,))] + [((chip,), (last,), 0) for chip in chips]
    lam = place_more(plan, lam, planes, [near] + late)
    lam, send = send_product(plan, lam, [(chips, (last,), 1)], [cross], staged)
    got = swap(send, "col", 1)
    keep = keep_product(plan, lam, staged)
    *near_parts, far_part = range(1, plan.n_pair)
    (word,) = code_sums(plan, [far_part], keep, got)
    words = [swap(word, "col", 2 * far_part)]
    mine, *coded = code_sums(plan, [0] + near_parts, keep, got)
    words += [swap(word, "col", 2 * m) for m, word in zip(near_parts, coded, strict=True)]
    return total_sums(plan, mine, words)


def solution(mesh):
    return jax.shard_map(
        shards,
        mesh=mesh,
        in_specs=(P(("row", "col"), None, None, None), P(("row", "col"), None), P("row", "col")),
        out_specs=P("col", "row"),
        check_vma=False,
    )
```

```python
import functools

import jax
import jax.numpy as jnp
from jax import lax
from jax.experimental import pallas as pl
from jax.experimental.pallas import tpu as pltpu
from jax.sharding import PartitionSpec as P

CAP = 16

VMEM = pl.BlockSpec(memory_space=pltpu.VMEM)
HBM = pl.BlockSpec(memory_space=pltpu.HBM)


def shift_of(size):
    assert size & (size - 1) == 0
    return size.bit_length() - 1


class Plan:
    def __init__(self, lam_tiles, integrals):
        self.n_row = lax.axis_size("row")
        self.n_col = lax.axis_size("col")
        g_dev, self.slots, self.pairs, self.tile = lam_tiles.shape
        assert g_dev == 1 and self.pairs == 16 and self.slots <= self.tile
        self.ab, self.cd = integrals.shape
        self.kt = self.cd // self.tile
        self.n_pair = self.n_col // 2
        self.per_row = self.n_col // self.n_row
        assert self.per_row % 2 == 0
        self.owned = self.n_col * self.pairs // self.per_row
        self.height = self.n_col * self.pairs
        self.bucket = (CAP + 1) * self.pairs
        self.head = -(-(self.n_col + 1) // 16) * 16
        self.body = self.slots * self.pairs
        self.packed = self.body + self.head


def pack_kernel(plan, ids, tiles, packed, ids_row, sem):
    load = pltpu.make_async_copy(tiles, packed.at[pl.ds(0, plan.body)], sem.at[0])
    load_ids = pltpu.make_async_copy(ids, ids_row, sem.at[1])
    load_ids.start()
    load.start()
    load_ids.wait()
    n = plan.slots
    row = jnp.broadcast_to(ids_row[...], (n, n))
    col = row.astype(jnp.float32).T.astype(jnp.int32)
    here, there = (lax.broadcasted_iota(jnp.int32, (n, n), i) for i in range(2))
    same = (row >> shift_of(plan.kt)) == (col >> shift_of(plan.kt))
    place_row = jnp.sum(jnp.where(same & (here < there), 1, 0), axis=0, keepdims=True)
    place_col = jnp.sum(jnp.where(same & (there < here), 1, 0), axis=1, keepdims=True)
    line = lax.broadcasted_iota(jnp.int32, (plan.head, n), 0)
    ids_line = jnp.broadcast_to(ids_row[...], (plan.head, n))
    block = ids_line >> shift_of(plan.kt)
    lane = lax.broadcasted_iota(jnp.int32, (n, plan.tile), 1)
    tile_at = lax.broadcasted_iota(jnp.int32, (n, plan.tile), 0)

    def spread(values, where):
        return lax.dot_general(
            values.astype(jnp.float32).astype(jnp.bfloat16),
            jnp.where(where, 1.0, 0.0).astype(jnp.bfloat16),
            (((1,), (0,)), ((), ())),
            preferred_element_type=jnp.float32,
        )

    missing = jnp.where(block == line, (ids_line & (plan.kt - 1)) - plan.kt, 0)
    places = spread(missing, place_col == lane) + plan.kt
    slot = jnp.where(line == plan.n_col, block * CAP + place_row, 0)
    slots = spread(slot, tile_at == lane)
    top = lax.broadcasted_iota(jnp.int32, (plan.head, plan.tile), 0)
    head = jnp.where(top == plan.n_col, slots, places)
    packed[plan.body :, :] = head.astype(jnp.bfloat16)
    load.wait()


def pack(plan, ids, tiles):
    ids, tiles = (pltpu.with_memory_space_constraint(x, pltpu.HBM) for x in (ids, tiles))
    return pl.pallas_call(
        functools.partial(pack_kernel, plan),
        out_shape=pltpu.VMEM((plan.packed, plan.tile), jnp.bfloat16),
        in_specs=[HBM, HBM],
        out_specs=VMEM,
        scratch_shapes=[
            pltpu.VMEM(ids.shape, jnp.int32),
            pltpu.SemaphoreType.DMA((2,)),
        ],
        compiler_params=pltpu.CompilerParams(vmem_limit_bytes=8 * 1024 * 1024),
        cost_estimate=cost(plan, 2 * plan.packed * plan.tile * 2),
        name="pack_tiles",
    )(ids, tiles)


def cost(plan, moved, flops=0):
    return pl.CostEstimate(flops=flops, bytes_accessed=moved, transcendentals=0)


def bucket_kernel(plan, count, both, *rest):
    packed, (buf, bodies, tops, heads, line, places, sem) = rest[:count], rest[count:]
    rows, piece = plan.pairs, (2 if both else count) * plan.bucket
    loads = []
    for i, ref in enumerate(packed):
        top = tops.at[pl.ds(i * plan.head, plan.head)]
        loads.append(pltpu.make_async_copy(ref.at[pl.ds(plan.body, plan.head)], top, sem.at[2 * i]))
        loads[-1].start()
    for i, ref in enumerate(packed):
        body = bodies.at[pl.ds(i * plan.body, plan.body)]
        loads.append(pltpu.make_async_copy(ref.at[pl.ds(0, plan.body)], body, sem.at[2 * i + 1]))
        loads[-1].start()
    col = lax.axis_index("col")
    for i in range(count):
        loads[i].wait()
        head = tops[i * plan.head : (i + 1) * plan.head, :].astype(jnp.float32)
        heads[i * plan.head : (i + 1) * plan.head, :] = head
        slot = head[plan.n_col : plan.n_col + 1, :].astype(jnp.int32)
        m = (slot >> shift_of(CAP)) ^ col
        at = (m >> 1) * piece + (slot & (CAP - 1)) * rows
        if both:
            line[i : i + 1, :] = at + (m & 1) * plan.bucket
        else:
            line[i : i + 1, :] = jnp.where((m & 1) == 0, at + i * plan.bucket, plan.n_pair * piece)
    copy = pltpu.make_async_copy(line, places, sem.at[2 * count])
    copy.start()
    for i in range(2 if both else count):
        for chip in range(plan.n_pair):
            at_line = (col ^ (2 * chip + i)) if both else i * plan.head + (col ^ (2 * chip))
            ids = heads[pl.ds(at_line, 1), :]
            at = chip * piece + i * plan.bucket + CAP * rows
            buf[at : at + rows, :] = jnp.broadcast_to(ids, (rows, plan.tile)).astype(jnp.bfloat16)
    copy.wait()
    for i in range(count):
        loads[count + i].wait()

        def step(s, _, i=i):
            at = pl.multiple_of(places[i, s], rows)
            tile = bodies[pl.ds(pl.multiple_of(i * plan.body + s * rows, rows), rows), :]
            buf[pl.ds(at, rows), :] = tile
            return 0

        lax.fori_loop(0, plan.slots, step, 0, unroll=16)


def bucket(plan, packed, both=False):
    count = len(packed)
    piece = (2 if both else count) * plan.bucket
    lines = -(-count // 8) * 8
    bf16 = jnp.bfloat16
    out = pl.pallas_call(
        functools.partial(bucket_kernel, plan, count, both),
        out_shape=pltpu.VMEM((plan.n_pair * piece + plan.pairs, plan.tile), bf16),
        in_specs=[HBM] * count,
        out_specs=VMEM,
        scratch_shapes=[
            pltpu.VMEM((count * plan.body, plan.tile), bf16),
            pltpu.VMEM((count * plan.head, plan.tile), bf16),
            pltpu.VMEM((count * plan.head, plan.tile), jnp.float32),
            pltpu.VMEM((lines, plan.tile), jnp.int32),
            pltpu.SMEM((lines, plan.tile), jnp.int32),
            pltpu.SemaphoreType.DMA((2 * count + 1,)),
        ],
        compiler_params=pltpu.CompilerParams(vmem_limit_bytes=12 * 1024 * 1024),
        cost_estimate=cost(plan, 4 * plan.n_pair * piece * plan.tile * 2),
        name="bucket_tiles",
    )(*packed)
    return [out[i * piece : (i + 1) * piece] for i in range(plan.n_pair)]


def place(plan, planes, parts, lam, tiles, line, places, sem, part_sem):
    rows = plan.pairs
    half = plan.n_pair * plan.owned
    sources, loads, at = [], [], 0
    for ref, (chips, ds, *sides) in zip(parts, planes, strict=True):
        sides = sides or (0, 1)
        size = len(chips) * len(ds) * len(sides) * plan.bucket
        here = tiles.at[pl.ds(at, size)]
        loads.append(pltpu.make_async_copy(ref.at[pl.ds(0, size)], here, part_sem.at[len(loads)]))
        loads[-1].start()
        for chip in chips:
            for d in ds:
                for side in sides:
                    sources.append((at, d, 2 * chip + side))
                    at += plan.bucket
    yield
    for load in loads:
        load.wait()
    for i, (base, _, _) in enumerate(sources):
        head = tiles[base + CAP * rows : base + plan.bucket, :].astype(jnp.float32)
        line[i : i + 1, :] = head[0:1, :].astype(jnp.int32)
    copy = pltpu.make_async_copy(line, places, sem)
    copy.start()
    copy.wait()
    row, col = lax.axis_index("row"), lax.axis_index("col")
    per_owner = plan.owned // rows
    for i, (base, d, m) in enumerate(sources):
        group = (row ^ d) * plan.n_col + (col ^ m)
        rel = (group >> shift_of(per_owner)) ^ col
        to = (rel & 1) * half + (rel >> 1) * plan.owned + (group & (per_owner - 1)) * rows
        for s in range(CAP):
            at = places[i, s]
            line_at = pl.multiple_of(jnp.where(at < plan.kt, to, 2 * half), rows)
            at = pl.multiple_of((at & (plan.kt - 1)) * plan.tile, plan.tile)
            tile = tiles[base + s * rows : base + (s + 1) * rows, :]
            lam[pl.ds(line_at, rows), pl.ds(at, plan.tile)] = tile
    yield


def place_scratch(plan, planes):
    count = sum(len(chips) * len(ds) * len(sides or (0, 1)) for chips, ds, *sides in planes)
    lines = -(-count // 8) * 8
    return [
        pltpu.VMEM((count * plan.bucket, plan.tile), jnp.bfloat16),
        pltpu.VMEM((lines, plan.tile), jnp.int32),
        pltpu.SMEM((lines, plan.tile), jnp.int32),
        pltpu.SemaphoreType.DMA,
        pltpu.SemaphoreType.DMA((len(planes),)),
    ]


def lam_shape(plan):
    return pltpu.VMEM((2 * plan.n_pair * plan.owned + plan.pairs, plan.cd), jnp.bfloat16)


def stage_kernel(plan, block, integrals, staged, sem):
    copies = []
    for i in range(plan.ab // block):
        here = pl.ds(i * block, block)
        copies.append(pltpu.make_async_copy(integrals.at[here], staged.at[here], sem.at[i]))
        copies[-1].start()
    for copy in copies:
        copy.wait()


def stage(plan, integrals, block=256):
    integrals = pltpu.with_memory_space_constraint(integrals, pltpu.HBM)
    return pl.pallas_call(
        functools.partial(stage_kernel, plan, block),
        out_shape=pltpu.VMEM(integrals.shape, integrals.dtype),
        in_specs=[HBM],
        out_specs=VMEM,
        scratch_shapes=[pltpu.SemaphoreType.DMA((plan.ab // block,))],
        compiler_params=pltpu.CompilerParams(vmem_limit_bytes=2 * 1024 * 1024),
        cost_estimate=cost(plan, 2 * plan.ab * plan.cd * 2),
        name="stage_integrals",
    )(integrals)


def early_kernel(plan, planes, *rest):
    parts, (lam, *scratch) = rest[: len(planes)], rest[len(planes) :]
    placing = place(plan, planes, parts, lam, *scratch)
    next(placing)
    lam[...] = jnp.zeros(lam.shape, lam.dtype)
    next(placing)


def place_early(plan, planes, parts):
    return pl.pallas_call(
        functools.partial(early_kernel, plan, planes),
        out_shape=lam_shape(plan),
        in_specs=[HBM] * len(parts),
        out_specs=VMEM,
        scratch_shapes=place_scratch(plan, planes),
        compiler_params=pltpu.CompilerParams(vmem_limit_bytes=12 * 1024 * 1024),
        cost_estimate=cost(plan, 4 * 1024 * 1024),
        name="place_early",
    )(*parts)


def more_kernel(plan, planes, _, *rest):
    parts, (lam, *scratch) = rest[: len(planes)], rest[len(planes) :]
    placing = place(plan, planes, parts, lam, *scratch)
    next(placing)
    next(placing)


def place_more(plan, lam, planes, parts):
    return pl.pallas_call(
        functools.partial(more_kernel, plan, planes),
        out_shape=lam_shape(plan),
        in_specs=[VMEM] + [HBM] * len(parts),
        out_specs=VMEM,
        input_output_aliases={0: 0},
        scratch_shapes=place_scratch(plan, planes),
        compiler_params=pltpu.CompilerParams(vmem_limit_bytes=12 * 1024 * 1024),
        cost_estimate=cost(plan, 4 * 1024 * 1024),
        name="place_more",
    )(lam, *parts)


def send_kernel(plan, planes, block, _, cols, *rest):
    parts, (lam, send, *scratch) = rest[: len(planes)], rest[len(planes) :]
    placing = place(plan, planes, parts, lam, *scratch)
    next(placing)
    next(placing)
    multiply(plan, block, lam, plan.n_pair * plan.owned, cols, send)


def send_product(plan, lam, planes, parts, integrals, block=256):
    half = plan.n_pair * plan.owned
    return pl.pallas_call(
        functools.partial(send_kernel, plan, planes, block),
        out_shape=[lam_shape(plan), pltpu.VMEM((half, plan.ab), jnp.float32)],
        in_specs=[VMEM, VMEM] + [HBM] * len(parts),
        out_specs=[VMEM, VMEM],
        input_output_aliases={0: 0},
        scratch_shapes=place_scratch(plan, planes),
        compiler_params=pltpu.CompilerParams(vmem_limit_bytes=20 * 1024 * 1024),
        cost_estimate=cost(plan, plan.ab * plan.cd * 4, 4 * half * plan.ab * plan.cd),
        name="place_and_multiply",
    )(lam, integrals, *parts)


def multiply(plan, block, lam, first, cols, out):
    for i in range(0, plan.ab, block):
        out[:, i : i + block] = lax.dot_general(
            lam[first : first + out.shape[0], :],
            cols[i : i + block, :],
            (((1,), (1,)), ((), ())),
            preferred_element_type=jnp.float32,
        )


def keep_kernel(plan, block, lam, cols, out):
    multiply(plan, block, lam, 0, cols, out)


def keep_product(plan, lam, integrals, block=256):
    half = plan.n_pair * plan.owned
    return pl.pallas_call(
        functools.partial(keep_kernel, plan, block),
        out_shape=pltpu.VMEM((half, plan.ab), jnp.float32),
        in_specs=[VMEM, VMEM],
        out_specs=VMEM,
        compiler_params=pltpu.CompilerParams(vmem_limit_bytes=20 * 1024 * 1024),
        cost_estimate=cost(plan, (plan.ab + half) * plan.cd * 2, 2 * half * plan.ab * plan.cd),
        name="multiply_kept",
    )(lam, integrals)


def chunks_of(plan):
    return plan.ab // plan.tile


def words_shape(plan):
    return (chunks_of(plan) // 2 * plan.owned + chunks_of(plan), plan.tile)


def code_kernel(plan, parts, keep, got, *rest):
    *words, square = rest
    rows, tile, chunks = plan.owned, plan.tile, chunks_of(plan)
    lane = lax.broadcasted_iota(jnp.int32, (rows, tile), 1)
    square[...] = jnp.zeros(square.shape, jnp.float32)
    for m, out in zip(parts, words, strict=True):
        here = slice(m * rows, (m + 1) * rows)
        if not m:
            out[...] = keep[here, :] + got[here, :]
            continue
        cells = [slice(j * tile, (j + 1) * tile) for j in range(chunks)]
        sums = [keep[here, cell] + got[here, cell] for cell in cells]
        most = jnp.zeros((rows, tile), jnp.float32)
        for j, part in enumerate(sums):
            most = jnp.where(lane == j, jnp.max(jnp.abs(part), axis=1, keepdims=True), most)
        power = jnp.floor(jnp.log2(jnp.maximum(most, 2.0**-106)) + 1.001)
        square[:rows, :] = power
        scale = jnp.exp2(15.0 - power)
        counts = []
        for j, part in enumerate(sums):
            count = jnp.floor(part * scale[:, j : j + 1] + 0.5)
            counts.append(jnp.clip(count, -32767.0, 32767.0).astype(jnp.int32))
        for j in range(chunks // 2):
            word = (counts[j] << 16) | (counts[j + chunks // 2] & 65535)
            out[j * rows : (j + 1) * rows, :] = word
        out[chunks // 2 * rows :, :] = square[...].T[:chunks, :].astype(jnp.int32)


def code_sums(plan, parts, keep, got):
    block = pltpu.VMEM((plan.owned, plan.ab), jnp.float32)
    coded = pltpu.VMEM(words_shape(plan), jnp.int32)
    return pl.pallas_call(
        functools.partial(code_kernel, plan, parts),
        out_shape=[coded if m else block for m in parts],
        in_specs=[VMEM] * 2,
        out_specs=[VMEM] * len(parts),
        scratch_shapes=[pltpu.VMEM((plan.tile, plan.tile), jnp.float32)],
        compiler_params=pltpu.CompilerParams(vmem_limit_bytes=20 * 1024 * 1024),
        cost_estimate=cost(plan, 4 * plan.n_pair * plan.owned * plan.ab * 4),
        name="code_sums",
    )(keep, got)


def total_kernel(plan, mine, *rest):
    words, (out, sums, square, sem) = rest[:-4], rest[-4:]
    rows, tile, chunks = plan.owned, plan.tile, chunks_of(plan)
    square[...] = jnp.zeros(square.shape, jnp.float32)
    scales = []
    for ref in words:
        square[:chunks, :] = ref[chunks // 2 * rows :, :].astype(jnp.float32)
        scales.append(jnp.exp2(square[...].T[:rows, :] - 16.0))
    copies = []
    for j in range(chunks):
        cell = slice(j * tile, (j + 1) * tile)
        at = j % (chunks // 2) * rows
        total = 0.5 * mine[:, cell]
        for ref, scale in zip(words, scales, strict=True):
            word = ref[at : at + rows, :]
            count = (word if j < chunks // 2 else word << 16) >> 16
            total += count.astype(jnp.float32) * scale[:, j : j + 1]
        sums[:, cell] = total
        copies.append(pltpu.make_async_copy(sums.at[:, cell], out.at[:, cell], sem.at[j]))
        copies[-1].start()
    for copy in copies:
        copy.wait()


def add_kernel(plan, mine, word, out, square):
    rows, tile, chunks = plan.owned, plan.tile, chunks_of(plan)
    square[...] = jnp.zeros(square.shape, jnp.float32)
    square[:chunks, :] = word[chunks // 2 * rows :, :].astype(jnp.float32)
    scale = jnp.exp2(square[...].T[:rows, :] - 15.0)
    for j in range(chunks):
        cell = slice(j * tile, (j + 1) * tile)
        at = j % (chunks // 2) * rows
        part = word[at : at + rows, :]
        count = (part if j < chunks // 2 else part << 16) >> 16
        out[:, cell] = mine[:, cell] + count.astype(jnp.float32) * scale[:, j : j + 1]


def add_sums(plan, mine, word):
    return pl.pallas_call(
        functools.partial(add_kernel, plan),
        out_shape=pltpu.VMEM(mine.shape, jnp.float32),
        in_specs=[VMEM] * 2,
        out_specs=VMEM,
        scratch_shapes=[pltpu.VMEM((plan.tile, plan.tile), jnp.float32)],
        compiler_params=pltpu.CompilerParams(vmem_limit_bytes=20 * 1024 * 1024),
        cost_estimate=cost(plan, 4 * plan.owned * plan.ab * 4),
        name="add_sums",
    )(mine, word)


def total_sums(plan, mine, words):
    return pl.pallas_call(
        functools.partial(total_kernel, plan),
        out_shape=jax.ShapeDtypeStruct((plan.owned, plan.ab), jnp.float32),
        in_specs=[VMEM] * (1 + len(words)),
        out_specs=HBM,
        scratch_shapes=[
            pltpu.VMEM((plan.owned, plan.ab), jnp.float32),
            pltpu.VMEM((plan.tile, plan.tile), jnp.float32),
            pltpu.SemaphoreType.DMA((chunks_of(plan),)),
        ],
        compiler_params=pltpu.CompilerParams(vmem_limit_bytes=20 * 1024 * 1024),
        cost_estimate=cost(plan, 4 * plan.n_pair * plan.owned * plan.ab * 4),
        name="total_sums",
    )(mine, *words)


def swap(x, axis, m):
    return lax.ppermute(x, axis, [(i, i ^ m) for i in range(lax.axis_size(axis))])


def shards(lam_tiles, lam_ids, integrals):
    plan = Plan(lam_tiles, integrals)
    packed = pack(plan, lam_ids, lam_tiles.reshape(plan.body, plan.tile))
    chips = range(plan.n_pair)

    def spread(ds):
        out = bucket(plan, [raw for d in ds for raw in (arrived[d], swap(arrived[d], "col", 1))])
        return [out[0]] + [swap(out[m], "col", 2 * m) for m in range(1, plan.n_pair)]

    bit = plan.n_row // 2
    arrived = {0: packed, bit: swap(packed, "row", bit)}
    own = spread([0])
    staged = stage(plan, integrals)
    arrived[bit], own, staged = lax.optimization_barrier((arrived[bit], own, staged))
    while bit > 1:
        bit //= 2
        arrived.update({d | bit: swap(raw, "row", bit) for d, raw in arrived.items() if d or bit > 1})
    *middle, last = sorted(arrived)[1:]
    early = spread(middle)
    arrived[last], early[1] = lax.optimization_barrier((arrived[last], early[1]))
    near = swap(jnp.concatenate(own, axis=0), "row", 1)
    late = bucket(plan, [arrived[last]], both=True)
    late = [late[0]] + [swap(late[m], "col", 2 * m) for m in range(1, plan.n_pair)]
    lam = place_early(plan, [((chip,), (0,)) for chip in chips], own)
    lam = place_more(plan, lam, [((chip,), tuple(middle)) for chip in chips], early)
    late, lam, near = lax.optimization_barrier((late, lam, near))
    cross = swap(jnp.concatenate([part[plan.bucket :] for part in late], axis=0), "col", 1)
    planes = [(chips, (1,))] + [((chip,), (last,), 0) for chip in chips]
    lam = place_more(plan, lam, planes, [near] + late)
    lam, send = send_product(plan, lam, [(chips, (last,), 1)], [cross], staged)
    got = swap(send, "col", 1)
    keep = keep_product(plan, lam, staged)
    *near_parts, far_part = range(1, plan.n_pair)
    (word,) = code_sums(plan, [far_part], keep, got)
    words = [swap(word, "col", 2 * far_part)]
    mine, *coded = code_sums(plan, [0] + near_parts, keep, got)
    words += [swap(word, "col", 2 * m) for m, word in zip(near_parts, coded, strict=True)]
    return total_sums(plan, add_sums(plan, mine, words[0]), words[1:])


def solution(mesh):
    return jax.shard_map(
        shards,
        mesh=mesh,
        in_specs=(P(("row", "col"), None, None, None), P(("row", "col"), None), P("row", "col")),
        out_specs=P("col", "row"),
        check_vma=False,
    )
```
